512 devices in a mesh: dp: 4 (over x), fsdp: 128 (over y, z, core).
Axes of the slice: x: 4, y: 8, z: 8, core: 2. Of those that a mesh axis runs over, the one named last changes fastest.
Arguments:
- frames: bfloat16 [65536, 1280], P(('dp', 'fsdp')), may hold values from -6 to 6
- live_frame_count: int32 [512], P(('dp', 'fsdp')), may hold values from 1 to 128, 49152 in all
- encoder_norm_gain: bfloat16 [1280], replicated, may hold values from 0.099609375 to 1.8984375
- encoder_quantized: bfloat16 [1280, 1280], P('fsdp'), may hold values from -0.15625 to 0.15625
- encoder_block_scale: bfloat16 [1280, 20], P('fsdp'), may hold values from 0.5 to 2
- text_token_embedding: bfloat16 [49152, 5120], P(('dp', 'fsdp')), may hold values from -6 to 6
- live_text_count: int32 [512], P(('dp', 'fsdp')), may hold values from 1 to 96, 36864 in all
- decoder_norm_gain: bfloat16 [5120], replicated, may hold values from 0.099609375 to 1.8984375
- value_quantized: bfloat16 [5120, 1024], P('fsdp'), may hold values from -0.078125 to 0.078125
- value_block_scale: bfloat16 [5120, 16], P('fsdp'), may hold values from 0.5 to 2
- adapter_down_factor: bfloat16 [5120, 64], P('fsdp'), may hold values from -0.078125 to 0.078125
- adapter_up_factor: bfloat16 [1024, 64], replicated, may hold values from -0.375 to 0.375
- audio_value_gradient: bfloat16 [16384, 1024], P(('dp', 'fsdp')), may hold values from -6 to 6
- text_value_gradient: bfloat16 [49152, 1024], P(('dp', 'fsdp')), may hold values from -24 to 24
Outputs:
- audio_values: bfloat16 [16384, 1024], P(('dp', 'fsdp'))
- text_values: bfloat16 [49152, 1024], P(('dp', 'fsdp'))
- audio_grad: bfloat16 [16384, 5120], P(('dp', 'fsdp'))
- text_grad: bfloat16 [49152, 5120], P(('dp', 'fsdp'))
- grad_down: float32 [5120, 64], P('fsdp')
- up_factor_gradient: float32 [1024, 64], P('fsdp')
The draws below stay inside these ranges and needn't reach their ends.
All inputs are finite; a program needn't handle non-finite values. No bound on the sum of `live_frame_count` or of `live_text_count` on one device may be relied on, other than what follows from the above.
Results may differ from the reference program's by a relative error of at most 0.007.
Values may be sent and summed in bfloat16 or wider, within the bound.
A program may use at most 192 MiB of HBM per device.

```python
import math
import jax
import jax.numpy as jnp
import numpy as np
from jax import lax

DE = 1280
DECODER_WIDTH = 5120
KV_HEADS = 8
HEAD = 128
ADAPTER_RANK = 64
BLOCK = 64
FRAMES_DEV = 128
TEXT_DEV = 96
VALUE_WIDTH = 1024
FRAMES = 65536
AUDIO = 16384
TEXTS = 49152
DEVICES = 512


def raised(values, key, source, target, shards_of, factor):
    owner, partner = [(jnp.arange(values.shape[axis_at]) // (values.shape[axis_at] // shards_of)).reshape([-1 if axis == axis_at else 1 for axis in range(values.ndim)]) for axis_at in (source, target)]
    chosen = jax.random.permutation(key, shards_of)[partner]
    strong = (owner == chosen) | (owner == (partner + shards_of // 2) % shards_of)
    return jnp.where(strong, factor * values, values)


def level_of(own_key, dims, cuts, low, high):
    loudness, own = 1.0, jax.random.fold_in(own_key, 6)
    for axis_at, parts in cuts:
        heights = jnp.exp(jax.random.uniform(jax.random.fold_in(own, axis_at), (parts,), jnp.float32, low / len(cuts), high / len(cuts)))
        loudness = loudness * jnp.repeat(heights, dims[axis_at] // parts).reshape([-1 if axis == axis_at else 1 for axis in range(len(dims))])
    return loudness


def profile(count, total, reach, slope):
    portions = [(1 << 20) // math.isqrt(standing ** slope) + 1 for standing in range(2, count + 1)]
    spare, counts = total - reach - (count - 1), [1] * (count - 1)
    while spare > 0:
        candidates = [i for i in range(count - 1) if counts[i] < reach]
        mass, budget = sum([portions[i] for i in candidates]), spare
        for i in candidates:
            more = min(reach - counts[i], max(1, budget * portions[i] // mass), spare)
            counts[i] = counts[i] + more
            spare = spare - more
    return np.array([reach] + counts)


def uneven(stream_key, amount, total, bound, skew):
    if amount == 2:
        one = jax.random.randint(stream_key, (), max(1, total - bound), min(bound, total - 1) + 1)
        return jnp.stack([one, total - one])
    sizes = jnp.asarray(profile(amount, total, bound, skew), jnp.int32)
    pairs = (amount - 1) // 2
    source_of, sink = sizes[1:1 + 2 * pairs:2], sizes[2:2 + 2 * pairs:2]
    margin = jnp.minimum(source_of - 1, bound - sink)
    moved = jax.random.randint(jax.random.fold_in(stream_key, 1), (pairs,), 0, 1 << 20) % (margin + 1)
    sizes = sizes.at[1:1 + 2 * pairs:2].set(source_of - moved).at[2:2 + 2 * pairs:2].set(sink + moved)
    return sizes[jax.random.permutation(jax.random.fold_in(stream_key, 2), amount)]


def scatter_about(stream_key, dims, spread, bound, shards=(), held_as=jnp.bfloat16):
    values = spread * jax.random.normal(stream_key, dims, jnp.float32)
    if shards:
        values = values * level_of(stream_key, dims, shards, -0.22, 0.18)
    return jnp.clip(values, -bound, bound).astype(held_as)


def bell_draw_with(key, shape, width, bound, cuts, heavy, held_as=jnp.bfloat16):
    values = width * jax.random.normal(key, shape, jnp.float32)
    if cuts:
        values = values * level_of(key, shape, cuts, -0.22, 0.18)
    return jnp.clip(raised(values, jax.random.fold_in(key, 3), *heavy), -bound, bound).astype(held_as)


def setup_inputs(seed: int = 0) -> dict:
    keys = jax.random.split(jax.random.key(seed), 15)
    return {
        "frames": scatter_about(keys[0], (FRAMES, DE), 1.0, 6.0, ((0, 512),)),
        "live_frame_count": uneven(keys[1], DEVICES, DEVICES * FRAMES_DEV * 3 // 4, FRAMES_DEV, 0).astype(jnp.int32),
        "encoder_norm_gain": jnp.clip(1.0 + 0.18 * jax.random.normal(keys[2], (DE,), jnp.float32), 0.099609375, 1.8984375).astype(jnp.bfloat16),
        "encoder_quantized": scatter_about(keys[3], (DE, DE), DE ** -0.5, 0.15625, ((0, 128),)),
        "encoder_block_scale": jnp.clip(jnp.exp(math.log(2.0) - 1.3862944 * jax.random.uniform(keys[4], (DE, DE // BLOCK), jnp.float32) ** level_of(keys[4], (DE, DE // BLOCK), ((0, 128),), -0.2, 0.2)), 0.5, 2.0).astype(jnp.bfloat16),
        "text_token_embedding": scatter_about(keys[5], (TEXTS, DECODER_WIDTH), 1.0, 6.0, ((0, 512),)),
        "live_text_count": uneven(keys[6], DEVICES, DEVICES * TEXT_DEV * 3 // 4, TEXT_DEV, 0).astype(jnp.int32),
        "decoder_norm_gain": jnp.clip(1.0 + 0.18 * jax.random.normal(keys[7], (DECODER_WIDTH,), jnp.float32), 0.099609375, 1.8984375).astype(jnp.bfloat16),
        "value_quantized": scatter_about(keys[8], (DECODER_WIDTH, VALUE_WIDTH), DECODER_WIDTH ** -0.5, 0.078125, ((0, 128),)),
        "value_block_scale": jnp.clip(jnp.exp(math.log(2.0) - 1.3862944 * jax.random.uniform(keys[9], (DECODER_WIDTH, VALUE_WIDTH // BLOCK), jnp.float32) ** level_of(keys[9], (DECODER_WIDTH, VALUE_WIDTH // BLOCK), ((0, 128),), -0.2, 0.2)), 0.5, 2.0).astype(jnp.bfloat16),
        "adapter_down_factor": scatter_about(keys[10], (DECODER_WIDTH, ADAPTER_RANK), DECODER_WIDTH ** -0.5, 0.078125, ((0, 128),)),
        "adapter_up_factor": scatter_about(keys[11], (VALUE_WIDTH, ADAPTER_RANK), (4 * ADAPTER_RANK) ** -0.5, 0.375),
        "audio_value_gradient": scatter_about(keys[12], (AUDIO, VALUE_WIDTH), 1.0, 6.0, ((0, 512),)),
        "text_value_gradient": bell_draw_with(keys[13], (TEXTS, VALUE_WIDTH), 1.0, 24.0, ((0, 512),), (0, 1, 512, 6.0)),
    }


adapter_scale = 2.0
epsilon = 1e-05

def dequant(packed, scales):
    height, breadth = packed.shape
    blocks = packed.astype(jnp.float32).reshape(height, breadth // BLOCK, BLOCK) * scales.astype(jnp.float32)[:, :, None]
    return blocks.reshape(height, breadth).astype(jnp.bfloat16)

def encode(frame_block, live, encoder_norm_gain, enc_weight):
    signal = frame_block.astype(jnp.float32)
    center = signal - lax.optimization_barrier(jnp.mean(signal, axis=1, keepdims=True))
    variance = lax.optimization_barrier(jnp.mean(center * center, axis=1, keepdims=True))
    normalized_input = (center * lax.rsqrt(variance + epsilon) * encoder_norm_gain.astype(jnp.float32)).astype(jnp.bfloat16)
    hidden = jnp.dot(normalized_input, enc_weight, preferred_element_type=jnp.float32)
    return ((signal + jax.nn.gelu(hidden, approximate=False)) * live[:, None]).astype(jnp.bfloat16)

def expand_blocks(input_rows, output_gradient, decoder_norm_gain, value_matrix, adapter_down_factor, adapter_up_factor):
    signal = input_rows.astype(jnp.float32)
    inverse = lax.rsqrt(lax.optimization_barrier(jnp.mean(signal * signal, axis=1, keepdims=True)) + epsilon)
    gains = decoder_norm_gain.astype(jnp.float32)
    normalized_input = (signal * inverse * gains).astype(jnp.bfloat16)
    adapter_hidden = jnp.dot(normalized_input, adapter_down_factor, preferred_element_type=jnp.float32).astype(jnp.bfloat16)
    value_output = jnp.dot(normalized_input, value_matrix, preferred_element_type=jnp.float32)
    value_output = value_output + adapter_scale * jnp.dot(adapter_hidden, adapter_up_factor.T, preferred_element_type=jnp.float32)
    lowrank_backward = (adapter_scale * jnp.dot(output_gradient, adapter_up_factor, preferred_element_type=jnp.float32)).astype(jnp.bfloat16)
    normed_gradient = jnp.dot(output_gradient, value_matrix.T, preferred_element_type=jnp.float32)
    normed_gradient = normed_gradient + jnp.dot(lowrank_backward, adapter_down_factor.T, preferred_element_type=jnp.float32)
    weighted = normed_gradient * gains
    cubed = inverse * inverse * inverse
    input_gradient = inverse * weighted - signal * cubed * lax.optimization_barrier(jnp.mean(weighted * signal, axis=1, keepdims=True))
    grad_down = jnp.dot(normalized_input.T, lowrank_backward, preferred_element_type=jnp.float32)
    up_factor_gradient = adapter_scale * jnp.dot(output_gradient.T, adapter_hidden, preferred_element_type=jnp.float32)
    return (value_output.astype(jnp.bfloat16), input_gradient.astype(jnp.bfloat16), grad_down, up_factor_gradient)

def reference(frames, live_frame_count, encoder_norm_gain, encoder_quantized, encoder_block_scale, text_token_embedding, live_text_count, decoder_norm_gain, value_quantized, value_block_scale, adapter_down_factor, adapter_up_factor, audio_value_gradient, text_value_gradient):
    enc_weight = dequant(encoder_quantized, encoder_block_scale)
    value_matrix = dequant(value_quantized, value_block_scale)
    groups = live_frame_count.shape[0]
    audio_rows = FRAMES_DEV // 4
    gradient_multiplier = 1.0 / math.sqrt(groups * (audio_rows + TEXT_DEV))
    frame_blocks = frames.reshape(groups, FRAMES_DEV, DE)
    text_blocks = text_token_embedding.reshape(groups, TEXT_DEV, DECODER_WIDTH)
    audio_cots = audio_value_gradient.reshape(groups, audio_rows, KV_HEADS * HEAD)
    text_cots = text_value_gradient.reshape(groups, TEXT_DEV, KV_HEADS * HEAD)

    def group_step(carry, item):
        frame_block, frame_live, text_block, text_live, audio_cot, text_cot = item
        live = (jnp.arange(FRAMES_DEV) < frame_live).astype(jnp.float32)
        encoded = encode(frame_block, live, encoder_norm_gain, enc_weight)
        audio = encoded.reshape(audio_rows, DECODER_WIDTH)
        input_rows = jnp.concatenate([audio, text_block], axis=0)
        text_mask = (jnp.arange(TEXT_DEV) < text_live).astype(text_cot.dtype)
        output_gradient = jnp.concatenate([audio_cot, text_cot * text_mask[:, None]], axis=0)
        value_output, input_gradient, partial_down_factor, partial_up_factor = expand_blocks(input_rows, output_gradient, decoder_norm_gain, value_matrix, adapter_down_factor, adapter_up_factor)
        carry = (carry[0] + partial_down_factor * gradient_multiplier, carry[1] + partial_up_factor * gradient_multiplier)
        return (carry, (value_output, input_gradient))
    start_carry = (jnp.zeros((DECODER_WIDTH, ADAPTER_RANK), jnp.float32), jnp.zeros((KV_HEADS * HEAD, ADAPTER_RANK), jnp.float32))
    sums, stacked = lax.scan(group_step, start_carry, (frame_blocks, live_frame_count, text_blocks, live_text_count, audio_cots, text_cots))
    value_output, input_gradient = stacked
    audio_values = value_output[:, :audio_rows].reshape(groups * audio_rows, KV_HEADS * HEAD)
    text_values = value_output[:, audio_rows:].reshape(groups * TEXT_DEV, KV_HEADS * HEAD)
    audio_grad = input_gradient[:, :audio_rows].reshape(groups * audio_rows, DECODER_WIDTH)
    text_grad = input_gradient[:, audio_rows:].reshape(groups * TEXT_DEV, DECODER_WIDTH)
    return (audio_values, text_values, audio_grad, text_grad, sums[0], sums[1])
```

```python
import math

import jax
import jax.numpy as jnp
import numpy as np
from jax import lax
from jax.experimental import pallas as pl
from jax.experimental.pallas import tpu as pltpu
from jax.sharding import PartitionSpec as P

MESH = pl.DeviceIdType.MESH
F32 = jnp.float32
BF16 = jnp.bfloat16

EPSILON = 1e-05
ADAPTER_SCALE = 2.0
X, Y, Z = 4, 8, 8
AUDIO_ROWS, TEXT_ROWS = 32, 96
ROWS = AUDIO_ROWS + TEXT_ROWS
ENC = 1280
HALF = ENC // 2
DEC = 5120
SLAB = DEC // Y
VALUE = 1024
RANK = 64
MULTIPLIER = 1.0 / math.sqrt(X * Y * Z * 2 * ROWS)

PEERS = (1, 7, 2, 6, 3, 5, 4)


def nn(a, b):
    return lax.dot_general(a, b, (((1,), (0,)), ((), ())), preferred_element_type=F32)


def nt(a, b):
    return lax.dot_general(a, b, (((1,), (1,)), ((), ())), preferred_element_type=F32)


def tn(a, b):
    return lax.dot_general(a, b, (((0,), (0,)), ((), ())), preferred_element_type=F32)


def one_hot(rows, columns, hit):
    i = lax.broadcasted_iota(jnp.int32, (rows, columns), 0)
    j = lax.broadcasted_iota(jnp.int32, (rows, columns), 1)
    return jnp.where(hit(i, j), 1.0, 0.0).astype(BF16)


def spread(blocks):
    return one_hot(blocks, blocks * 64, lambda i, j: (j >= 64 * i) & (j < 64 * i + 64))


def erf(x):
    x = jnp.clip(x, -3.832506856900711, 3.832506856900711)
    s = x * x
    p = jnp.full_like(s, 0.00022905065861350646)
    for k in (0.0034082910107109506, 0.050955695062380861, 0.18520832239976145, 1.128379143519084):
        p = p * s + k
    q = jnp.full_like(s, -1.1791602954361697e-7)
    for k in (
        0.000023547966471313185,
        0.0010179625278914885,
        0.014070470171167667,
        0.11098505178285362,
        0.49746925110067538,
        1.0,
    ):
        q = q * s + k
    return x * p / q


def kernel(
    frames, live_frames, enc_gain, enc_q, enc_s, text, live_text, dec_gain, val_q, val_s,
    down, up, audio_cot, text_cot, source,
    out_av, out_tv, out_ag, out_tg, out_gd, out_gu,
    V, E, DT, e1, dn1, ebuf, et, et2, wv, vx, cot, xs, nrm, gn, acc, enc_f, en_p,
    R1, R2, RZs, RZr, RYs, RYr, FX,
    pair_s, pair_r, p1v_s, p1v_r, p1e_s, p1e_r, p1d_s, p1d_r,
    er_s, er_r, ed_s, ed_r, dr_s, dr_r, dd_s, dd_r, vy_s, vy_r, vx_s, vx_r, vd_s, vd_r,
    rp_s, rp_r, rz_s, rz_r, ry_s, ry_r, rx_s, rx_r,
):
    x = lax.axis_index("dp")
    f = lax.axis_index("fsdp")
    c = f % 2
    z = (f // 2) % Z
    y = f // (2 * Z)
    par = x % 2
    oc = 1 - c

    def dev(dx=0, dy=0, dz=0, core=None):
        return (
            (x + dx) % X if dx else x,
            (((y + dy) % Y if dy else y) * Z + ((z + dz) % Z if dz else z)) * 2
            + (c if core is None else core),
        )

    sibling = dev(core=oc)
    sent = []

    def send(src, dst, ss, rs, to):
        copy = pltpu.make_async_remote_copy(
            src_ref=src, dst_ref=dst, send_sem=ss, recv_sem=rs, device_id=to, device_id_type=MESH
        )
        copy.start()
        sent.append(copy)

    def got(dst, ss, rs):
        pltpu.make_async_remote_copy(
            src_ref=dst, dst_ref=dst, send_sem=ss, recv_sem=rs, device_id=sibling,
            device_id_type=MESH,
        ).wait_recv()

    barrier = pltpu.get_barrier_semaphore()
    peers = [sibling]
    peers += [dev(dx=k) for k in range(1, X)]
    peers += [dev(dy=k) for k in range(1, Y)]
    peers += [dev(dz=k) for k in range(1, Z)]
    for peer in peers:
        pl.semaphore_signal(barrier, inc=1, device_id=peer, device_id_type=MESH)

    weight = val_q[...].astype(F32) * nn(val_s[...], spread(VALUE // 64))
    for b in range(8):
        wv[b // 4, b % 4] = weight[:, 128 * b : 128 * b + 128]
    et[...] = jnp.zeros_like(et)
    et[0:10, :] = enc_q[...].astype(F32) * nn(enc_s[...], spread(ENC // 64))
    for h in range(2):
        ebuf[h] = et[:, HALF * h : HALF * (h + 1)].astype(BF16)
    dn1[z, c] = nn(down[...], one_hot(RANK, 128, lambda i, j: i == j))
    vx[c] = wv[c, pl.ds(2 * par, 2)]
    e1[y, c] = ebuf[c]

    pl.semaphore_wait(barrier, len(peers))

    send(wv.at[oc, pl.ds(2 * par, 2)], vx.at[c], pair_s.at[0], pair_r.at[0], sibling)
    send(ebuf.at[oc], e1.at[y, c], pair_s.at[1], pair_r.at[1], sibling)
    send(dn1.at[z, c], dn1.at[z, c], pair_s.at[2], pair_r.at[2], sibling)

    got(vx.at[oc], pair_s.at[0], pair_r.at[0])
    for i in range(2):
        V[c, 2 * par + i, y, pl.ds(pl.multiple_of(80 * z, 16), 80), :] = jnp.concatenate(
            [vx[0, i], vx[1, i]], axis=0
        ).astype(BF16)

    def chip_rows(zz):
        return V.at[c, pl.ds(2 * par, 2), y, pl.ds(pl.multiple_of(80 * zz, 16), 80)]

    for k in PEERS:
        send(chip_rows(z), chip_rows(z), p1v_s.at[k], p1v_r.at[k], dev(dz=k))
    got(e1.at[y, oc], pair_s.at[1], pair_r.at[1])
    for k in PEERS:
        send(e1.at[y], e1.at[y], p1e_s.at[k], p1e_r.at[k], dev(dy=k))
    got(dn1.at[z, oc], pair_s.at[2], pair_r.at[2])
    for k in PEERS:
        send(dn1.at[z], dn1.at[z], p1d_s.at[k], p1d_r.at[k], dev(dz=k))

    signal = frames[...].astype(F32)
    center = signal - jnp.mean(signal, axis=1, keepdims=True)
    variance = jnp.mean(center * center, axis=1, keepdims=True)
    en = (center * lax.rsqrt(variance + EPSILON) * enc_gain[...].astype(F32)).astype(BF16)
    feature = lax.broadcasted_iota(jnp.int32, (ENC, 128), 0)
    for b in range(ENC // 128):
        cols = slice(128 * b, 128 * b + 128)
        pick = jnp.where(feature == source[:, cols], 1.0, 0.0).astype(BF16)
        en_p[:, cols] = nn(en, pick).astype(BF16)

    for k in PEERS:
        got(e1.at[(y + 8 - k) % Y], p1e_s.at[k], p1e_r.at[k])
    for yy in range(Y):
        for cc in range(2):
            et2[20 * yy + 10 * cc : 20 * yy + 10 * cc + 10, :] = e1[yy, cc].astype(F32)[0:10]
    E[c, z] = et2[...].astype(BF16)

    def e_slab(s, d, way):
        return E.at[c, s] if d < 3 else E.at[c, s, pl.ds(80 * way, 80)]

    def e_send(d):
        send(e_slab((z + 8 - d) % Z, d, 0), e_slab((z + 8 - d) % Z, d, 0), er_s.at[0, d], er_r.at[0, d], dev(dz=1))
        send(e_slab((z + d) % Z, d, 1), e_slab((z + d) % Z, d, 1), er_s.at[1, d], er_r.at[1, d], dev(dz=7))

    def e_share(s, n):
        send(E.at[c, s], E.at[c, s], ed_s.at[n], ed_r.at[n], sibling)

    def e_step(d):
        lo, hi = (z + 7 - d) % Z, (z + 1 + d) % Z
        got(e_slab(lo, d, 0), er_s.at[0, d], er_r.at[0, d])
        got(e_slab(hi, d, 1), er_s.at[1, d], er_r.at[1, d])
        if d < 3:
            e_send(d + 1)
            e_share(lo, 1 + 2 * d)
            e_share(hi, 2 + 2 * d)
        else:
            e_share(lo, 7)

    e_send(0)
    e_share(z, 0)

    for k in PEERS:
        got(chip_rows((z + 8 - k) % Z), p1v_s.at[k], p1v_r.at[k])

    def v_blk(s, i):
        return V.at[c, 2 * par + i, s]

    def x_blk(s, i):
        return V.at[c, 2 * (1 - par) + i, s]

    def v_send(way, d, i):
        s = (y + 8 - d) % Y if way == 0 else (y + d) % Y
        send(v_blk(s, i), v_blk(s, i), vy_s.at[way, d, i], vy_r.at[way, d, i], dev(dy=1 if way == 0 else 7))

    def v_spread(s, n, i):
        send(v_blk(s, i), v_blk(s, i), vx_s.at[i, n], vx_r.at[i, n], dev(dx=1 if i == 0 else 3))
        send(v_blk(s, i), v_blk(s, i), vd_s.at[n, i], vd_r.at[n, i], sibling)

    def v_step(d, i):
        for way in range(2):
            if d == 3 and way != i:
                continue
            s = (y + 7 - d) % Y if way == 0 else (y + 1 + d) % Y
            got(v_blk(s, i), vy_s.at[way, d, i], vy_r.at[way, d, i])
            if d < 2 or (d == 2 and way == i):
                v_send(way, d + 1, i)
            v_spread(s, 7 if d == 3 else 1 + 2 * d + way, i)

    def slab_of(n):
        d = (n + 1) // 2
        return (y + 8 - d) % Y if n % 2 == 1 else (y + d) % Y

    def x_step(n):
        s = slab_of(n)
        for i in range(2):
            got(x_blk(s, i), vx_s.at[i, n], vx_r.at[i, n])
            send(x_blk(s, i), x_blk(s, i), vd_s.at[n, 2 + i], vd_r.at[n, 2 + i], sibling)

    def ready(n):
        s = slab_of(n)
        for i in range(2):
            got(V.at[oc, 2 * par + i, s], vd_s.at[n, i], vd_r.at[n, i])
            got(V.at[oc, 2 * (1 - par) + i, s], vd_s.at[n, 2 + i], vd_r.at[n, 2 + i])

    for i in range(2):
        v_send(0, 0, i)
        v_send(1, 0, i)
        v_spread(y, 0, i)

    for k in PEERS:
        got(dn1.at[(z + 8 - k) % Z], p1d_s.at[k], p1d_r.at[k])
    turned = jnp.transpose(dn1[...].reshape(SLAB, 128))
    for h in range(2):
        DT[h, y] = turned[32 * h : 32 * h + 32, :].astype(BF16)

    def d_slab(s, d, way):
        return DT.at[c, s] if d < 3 else DT.at[c, s, pl.ds(16 * way, 16)]

    def d_send(d):
        send(d_slab((y + 8 - d) % Y, d, 0), d_slab((y + 8 - d) % Y, d, 0), dr_s.at[0, d], dr_r.at[0, d], dev(dy=1))
        send(d_slab((y + d) % Y, d, 1), d_slab((y + d) % Y, d, 1), dr_s.at[1, d], dr_r.at[1, d], dev(dy=7))

    def d_step(d):
        got(d_slab((y + 7 - d) % Y, d, 0), dr_s.at[0, d], dr_r.at[0, d])
        got(d_slab((y + 1 + d) % Y, d, 1), dr_s.at[1, d], dr_r.at[1, d])
        if d < 3:
            d_send(d + 1)

    d_send(0)

    cot[0:AUDIO_ROWS, :] = audio_cot[...]
    row = lax.broadcasted_iota(jnp.int32, (TEXT_ROWS, 1), 0)
    mask = jnp.where(row < live_text[...], 1.0, 0.0)
    cot[AUDIO_ROWS:ROWS, :] = (text_cot[...].astype(F32) * mask).astype(BF16)
    bl = (ADAPTER_SCALE * nn(cot[...], up[...])).astype(BF16)
    gains = [dec_gain[:, SLAB * k : SLAB * (k + 1)].astype(F32) for k in range(Y)]
    square = jnp.zeros((TEXT_ROWS, 1), F32)
    for k in range(Y):
        part = text[:, SLAB * k : SLAB * (k + 1)].astype(F32)
        square += jnp.sum(part * part, axis=1, keepdims=True)
    inv_text = lax.rsqrt(square * (1.0 / DEC) + EPSILON)
    for k in range(Y):
        part = text[:, SLAB * k : SLAB * (k + 1)].astype(F32)
        xs[k, AUDIO_ROWS:ROWS, :] = part
        nrm[k, AUDIO_ROWS:ROWS, :] = (part * inv_text * gains[k]).astype(BF16)

    def whole(s):
        return jnp.concatenate([V[b // 4, b % 4, s] for b in range(8)], axis=1)

    def backward(n):
        s = slab_of(n)
        gn[s] = nt(cot[...], whole(s))

    def forward(n):
        s = slab_of(n)
        product = nn(nrm[s], whole(s))
        acc[...] = product if n == 0 else acc[...] + product

    e_step(0)
    d_step(0)
    v_step(0, 0)
    x_step(0)
    e_step(1)
    d_step(1)
    v_step(0, 1)
    ready(0)
    backward(0)
    v_step(1, 0)
    e_step(2)
    d_step(2)
    d_step(3)
    send(DT.at[c], DT.at[c], dd_s.at[0], dd_r.at[0], sibling)
    x_step(1)
    x_step(2)
    e_step(3)
    v_step(1, 1)

    slab_at = [z] + [(z + 7 - n // 2) % Z if n % 2 == 0 else (z + 1 + n // 2) % Z for n in range(6)] + [(z + 4) % Z]
    for n in range(8):
        got(E.at[oc, slab_at[n]], ed_s.at[n], ed_r.at[n])
    frame = lax.broadcasted_iota(jnp.int32, (4 * AUDIO_ROWS, 1), 0)
    live = jnp.where(frame < live_frames[...], 1.0, 0.0)
    for h in range(2):
        cols = slice(HALF * h, HALF * (h + 1))
        hidden = nn(en_p[...], E[h].reshape(ENC, HALF))
        gelu = 0.5 * hidden * (1.0 + erf(hidden * (1.0 / math.sqrt(2.0))))
        encoded = ((frames[:, cols].astype(F32) + gelu) * live).astype(BF16)
        for b in range(5):
            enc_f[5 * h + b] = encoded[:, 128 * b : 128 * b + 128].astype(F32)
    square = jnp.zeros((AUDIO_ROWS, 1), F32)
    for k in range(4):
        for b in range(10):
            part = enc_f[b, pl.ds(k, AUDIO_ROWS, stride=4), :]
            square += jnp.sum(part * part, axis=1, keepdims=True)
            xs[2 * k + b // 5, 0:AUDIO_ROWS, 128 * (b % 5) : 128 * (b % 5) + 128] = part
    inv_audio = lax.rsqrt(square * (1.0 / DEC) + EPSILON)
    for k in range(Y):
        nrm[k, 0:AUDIO_ROWS, :] = (xs[k, 0:AUDIO_ROWS, :] * inv_audio * gains[k]).astype(BF16)

    got(DT.at[oc], dd_s.at[0], dd_r.at[0])
    low = jnp.zeros((ROWS, RANK), F32)
    for k in range(Y):
        low += nt(nrm[k], jnp.concatenate([DT[0, k], DT[1, k]], axis=0))
    lr = low.astype(BF16)
    twice = one_hot(RANK, 128, lambda i, j: (j == i) | (j == i + RANK))
    bl2 = nn(bl, twice).astype(BF16)
    lr2 = nn(lr, twice).astype(BF16)
    first = lax.broadcasted_iota(jnp.int32, (24, 128), 1) < RANK
    g_up = tn(cot[...], lr2) * (ADAPTER_SCALE * MULTIPLIER)
    for k in range(Y):
        g_down = tn(nrm[k], bl2) * MULTIPLIER
        for zz in range(Z):
            for cc in range(2):
                at = 80 * zz + 40 * cc
                u = 16 * (Z * k + zz) + 8 * cc
                tail = jnp.concatenate([g_down[at + 24 : at + 40], g_up[u : u + 8]], axis=0)
                R1[cc, zz, 24 * k : 24 * k + 24, :] = jnp.where(first, g_down[at : at + 24], tail)
    send(R1.at[oc], R2, rp_s.at[0], rp_r.at[0], sibling)

    v_step(2, 0)
    ready(1)
    ready(2)
    backward(1)
    got(R2, rp_s.at[0], rp_r.at[0])
    for zz in range(Z):
        RZs[zz] = (R1[c, zz] + R2[zz]).astype(BF16)
    for k in PEERS:
        send(RZs.at[(z + k) % Z], RZr.at[k], rz_s.at[k], rz_r.at[k], dev(dz=k))
    v_step(2, 1)
    backward(2)
    x_step(3)
    x_step(4)
    v_step(3, 0)
    v_step(3, 1)
    forward(0)
    forward(1)
    forward(2)
    ready(3)
    ready(4)
    backward(3)
    forward(3)
    x_step(5)
    x_step(6)
    backward(4)
    forward(4)

    total = RZs[z].astype(F32)
    for k in PEERS:
        got(RZr.at[k], rz_s.at[k], rz_r.at[k])
        total += RZr[k].astype(F32)
    for yy in range(Y):
        RYs[yy] = total[24 * yy : 24 * yy + 24]
    for k in PEERS:
        send(RYs.at[(y + k) % Y], RYr.at[k], ry_s.at[k], ry_r.at[k], dev(dy=k))

    ready(5)
    ready(6)
    backward(5)
    forward(5)
    x_step(7)
    backward(6)
    forward(6)

    total = RYs[y]
    for k in PEERS:
        got(RYr.at[k], ry_s.at[k], ry_r.at[k])
        total += RYr[k]
    FX[x] = total
    for k in range(1, X):
        send(FX.at[x], FX.at[x], rx_s.at[k], rx_r.at[k], dev(dx=k))

    ready(7)
    backward(7)
    forward(7)

    values = (acc[...] + ADAPTER_SCALE * nt(lr, up[...])).astype(BF16)
    out_av[...] = values[0:AUDIO_ROWS]
    out_tv[...] = values[AUDIO_ROWS:ROWS]
    inverse = jnp.concatenate([inv_audio, inv_text], axis=0)
    mean = jnp.zeros((ROWS, 1), F32)
    for k in range(Y):
        both = jnp.concatenate([DT[0, k], DT[1, k]], axis=0)
        u = (gn[k] + nn(bl, both)) * gains[k]
        gn[k] = u
        mean += jnp.sum(u * xs[k], axis=1, keepdims=True)
    scale = inverse * inverse * inverse * (mean * (1.0 / DEC))
    for k in range(Y):
        cols = slice(SLAB * k, SLAB * (k + 1))
        grad = (inverse * gn[k] - xs[k] * scale).astype(BF16)
        out_ag[:, cols] = grad[0:AUDIO_ROWS]
        out_tg[:, cols] = grad[AUDIO_ROWS:ROWS]

    for k in range(1, X):
        got(FX.at[(x + 4 - k) % X], rx_s.at[k], rx_r.at[k])
    total = FX[0] + FX[1] + FX[2] + FX[3]
    right = pltpu.roll(total, RANK, axis=1)
    out_gd[0:24, :] = total[:, :RANK]
    out_gd[24:40, :] = right[0:16, :RANK]
    out_gu[...] = right[16:24, :RANK]

    for copy in sent:
        copy.wait_send()


def natural_features():
    place = np.arange(ENC)
    return (160 * (place % 160 // 20) + 20 * (place // 160) + place % 20).astype(np.int32)[None]


def shards(
    frames, live_frames, enc_gain, enc_q, enc_s, text, live_text, dec_gain, val_q, val_s,
    down, up, audio_cot, text_cot,
):
    dma = pltpu.SemaphoreType.DMA
    vmem = pltpu.VMEM
    return pl.pallas_call(
        kernel,
        out_shape=(
            jax.ShapeDtypeStruct((AUDIO_ROWS, VALUE), BF16),
            jax.ShapeDtypeStruct((TEXT_ROWS, VALUE), BF16),
            jax.ShapeDtypeStruct((AUDIO_ROWS, DEC), BF16),
            jax.ShapeDtypeStruct((TEXT_ROWS, DEC), BF16),
            jax.ShapeDtypeStruct((40, RANK), F32),
            jax.ShapeDtypeStruct((8, RANK), F32),
        ),
        in_specs=[pl.BlockSpec(memory_space=vmem)] * 15,
        out_specs=[pl.BlockSpec(memory_space=vmem)] * 6,
        scratch_shapes=[
            vmem((2, 4, Y, SLAB, 128), BF16),
            vmem((2, Z, 160, HALF), BF16),
            vmem((2, Y, 32, SLAB), BF16),
            vmem((Y, 2, 16, HALF), BF16),
            vmem((Z, 2, 40, 128), F32),
            vmem((2, 16, HALF), BF16),
            vmem((16, ENC), F32),
            vmem((160, HALF), F32),
            vmem((2, 4, 40, 128), F32),
            vmem((2, 2, 40, 128), F32),
            vmem((ROWS, VALUE), BF16),
            vmem((Y, ROWS, SLAB), F32),
            vmem((Y, ROWS, SLAB), BF16),
            vmem((Y, ROWS, SLAB), F32),
            vmem((ROWS, VALUE), F32),
            vmem((ENC // 128, 4 * AUDIO_ROWS, 128), F32),
            vmem((4 * AUDIO_ROWS, ENC), BF16),
            vmem((2, Z, 24 * Y, 128), F32),
            vmem((Z, 24 * Y, 128), F32),
            vmem((Z, 24 * Y, 128), BF16),
            vmem((Z, 24 * Y, 128), BF16),
            vmem((Y, 24, 128), F32),
            vmem((Y, 24, 128), F32),
            vmem((X, 24, 128), F32),
        ]
        + [
            dma(shape)
            for shape in (
                (3,), (8,), (8,), (8,), (2, 4), (8,), (2, 4), (1,), (2, 4, 2), (2, 8), (8, 4),
                (1,), (8,), (8,), (4,),
            )
            for _ in range(2)
        ],
        compiler_params=pltpu.CompilerParams(
            collective_id=0, has_side_effects=True, vmem_limit_bytes=56 * 1024 * 1024
        ),
        cost_estimate=pl.CostEstimate(
            flops=2 * ROWS * (2 * DEC * VALUE + ENC * ENC), bytes_accessed=6_000_000, transcendentals=0
        ),
    )(
        frames,
        live_frames.reshape(1, 1),
        enc_gain.reshape(1, ENC),
        enc_q,
        enc_s,
        text,
        live_text.reshape(1, 1),
        dec_gain.reshape(1, DEC),
        val_q,
        val_s,
        down,
        up,
        audio_cot,
        text_cot,
        jnp.asarray(natural_features()),
    )


def solution(mesh):
    both = ("dp", "fsdp")
    in_specs = (
        P(both, None), P(both), P(), P("fsdp", None), P("fsdp", None), P(both, None), P(both), P(),
        P("fsdp", None), P("fsdp", None), P("fsdp", None), P(), P(both, None), P(both, None),
    )
    out_specs = (
        P(both, None), P(both, None), P(both, None), P(both, None), P("fsdp", None), P("fsdp", None),
    )
    return jax.shard_map(shards, mesh=mesh, in_specs=in_specs, out_specs=out_specs, check_vma=False)
```

```python
import math

import jax
import jax.numpy as jnp
import numpy as np
from jax import lax
from jax.experimental import pallas as pl
from jax.experimental.pallas import tpu as pltpu
from jax.sharding import PartitionSpec as P

MESH = pl.DeviceIdType.MESH
F32 = jnp.float32
BF16 = jnp.bfloat16

EPSILON = 1e-05
ADAPTER_SCALE = 2.0
X, Y, Z = 4, 8, 8
AUDIO_ROWS, TEXT_ROWS = 32, 96
ROWS = AUDIO_ROWS + TEXT_ROWS
ENC = 1280
HALF = ENC // 2
DEC = 5120
SLAB = DEC // Y
VALUE = 1024
RANK = 64
MULTIPLIER = 1.0 / math.sqrt(X * Y * Z * 2 * ROWS)

PEERS = (1, 7, 2, 6, 3, 5, 4)


def nn(a, b):
    return lax.dot_general(a, b, (((1,), (0,)), ((), ())), preferred_element_type=F32)


def nt(a, b):
    return lax.dot_general(a, b, (((1,), (1,)), ((), ())), preferred_element_type=F32)


def tn(a, b):
    return lax.dot_general(a, b, (((0,), (0,)), ((), ())), preferred_element_type=F32)


def one_hot(rows, columns, hit):
    i = lax.broadcasted_iota(jnp.int32, (rows, columns), 0)
    j = lax.broadcasted_iota(jnp.int32, (rows, columns), 1)
    return jnp.where(hit(i, j), 1.0, 0.0).astype(BF16)


def spread(blocks):
    return one_hot(blocks, blocks * 64, lambda i, j: (j >= 64 * i) & (j < 64 * i + 64))


def erf(x):
    x = jnp.clip(x, -3.832506856900711, 3.832506856900711)
    s = x * x
    p = jnp.full_like(s, 0.00022905065861350646)
    for k in (0.0034082910107109506, 0.050955695062380861, 0.18520832239976145, 1.128379143519084):
        p = p * s + k
    q = jnp.full_like(s, -1.1791602954361697e-7)
    for k in (
        0.000023547966471313185,
        0.0010179625278914885,
        0.014070470171167667,
        0.11098505178285362,
        0.49746925110067538,
        1.0,
    ):
        q = q * s + k
    return x * p / q


def kernel(
    *refs,
):
    given, refs = refs[:15], refs[15:]
    out_av, out_tv, out_ag, out_tg, out_gd, out_gu = refs[:6]
    held, refs = refs[6:21], refs[21:]
    (
        frames, live_frames, enc_gain, enc_q, enc_s, text, live_text, dec_gain, val_q, val_s,
        down, up, audio_cot, text_cot, source,
    ) = held
    (
    V, E, DT, e1, dnp, tdn, dn1, ebuf, emine, et, et2, wv, vx, cot, xs, nrm, gn, acc, enc_f, en_p,
    hall, hbuf,
    R1, R2, RZs, RZr, RYs, RYr, FX,
    in_sem, pair_s, pair_r, p1v_s, p1v_r, p1e_s, p1e_r, p1d_s, p1d_r,
    er_s, er_r, ex_s, ex_r, hp_s, hp_r, dr_s, dr_r, dd_s, dd_r, vy_s, vy_r, vx_s, vx_r, vd_s, vd_r,
    rp_s, rp_r, rz_s, rz_r, ry_s, ry_r, rx_s, rx_r,
    ) = refs
    x = lax.axis_index("dp")
    f = lax.axis_index("fsdp")
    c = f % 2
    z = (f // 2) % Z
    y = f // (2 * Z)
    par = x % 2
    oc = 1 - c

    def dev(dx=0, dy=0, dz=0, core=None):
        return (
            (x + dx) % X if dx else x,
            (((y + dy) % Y if dy else y) * Z + ((z + dz) % Z if dz else z)) * 2
            + (c if core is None else core),
        )

    sibling = dev(core=oc)
    sent = []

    def send(src, dst, ss, rs, to):
        copy = pltpu.make_async_remote_copy(
            src_ref=src, dst_ref=dst, send_sem=ss, recv_sem=rs, device_id=to, device_id_type=MESH
        )
        copy.start()
        sent.append(copy)

    def got(dst, ss, rs):
        pltpu.make_async_remote_copy(
            src_ref=dst, dst_ref=dst, send_sem=ss, recv_sem=rs, device_id=sibling,
            device_id_type=MESH,
        ).wait_recv()

    barrier = pltpu.get_barrier_semaphore()
    peers = [sibling]
    peers += [dev(dx=k) for k in range(1, X)]
    peers += [dev(dy=k, core=core) for k in range(1, Y) for core in (c, oc)]
    peers += [dev(dz=k) for k in range(1, Z)]
    for peer in peers:
        pl.semaphore_signal(barrier, inc=1, device_id=peer, device_id_type=MESH)

    loads = [pltpu.make_async_copy(given[i], held[i], in_sem.at[i]) for i in range(15)]
    for i in (9, 8, 4, 3, 10, 0, 2, 14, 13, 12, 11, 6, 5, 7, 1):
        loads[i].start()

    def loaded(*indices):
        for i in indices:
            loads[i].wait()

    def e_index(r):
        return 2 if r == 2 else 3 * par + r

    loaded(9, 8)
    weight = val_q[...].astype(F32) * tn(val_s[...], spread(VALUE // 64))
    for b in range(8):
        wv[b // 4, b % 4] = weight[:, 128 * b : 128 * b + 128]
    et[...] = jnp.zeros_like(et)
    loaded(4, 3)
    et[0:10, :] = enc_q[...].astype(F32) * nn(enc_s[...], spread(ENC // 64))
    for b in range(10):
        ebuf[b // 5, b % 5] = et[:, 128 * b : 128 * b + 128].astype(BF16)
    for h in range(2):
        for r in range(3):
            emine[h, r] = ebuf[h, e_index(r)]
    loaded(10)
    dnp[c] = nn(down[...], one_hot(RANK, 128, lambda i, j: i == j))
    tdn[...] = jnp.zeros_like(tdn)
    vx[c] = wv[c, pl.ds(2 * par, 2)]
    e1[y, c] = emine[c]

    pl.semaphore_wait(barrier, len(peers))

    send(wv.at[oc, pl.ds(2 * par, 2)], vx.at[c], pair_s.at[0], pair_r.at[0], sibling)
    send(emine.at[oc], e1.at[y, c], p1e_s.at[0, 1], p1e_r.at[0, 1], sibling)
    for k in PEERS:
        send(emine.at[c], e1.at[y, c], p1e_s.at[k, 0], p1e_r.at[k, 0], dev(dy=k))
        send(emine.at[oc], e1.at[y, c], p1e_s.at[k, 1], p1e_r.at[k, 1], dev(dy=k, core=oc))
    send(dnp.at[c], dnp.at[c], pair_s.at[1], pair_r.at[1], sibling)

    got(vx.at[oc], pair_s.at[0], pair_r.at[0])
    for i in range(2):
        V[c, 2 * par + i, y, pl.ds(pl.multiple_of(80 * z, 16), 80), :] = jnp.concatenate(
            [vx[0, i], vx[1, i]], axis=0
        ).astype(BF16)

    def chip_rows(zz):
        return V.at[c, pl.ds(2 * par, 2), y, pl.ds(pl.multiple_of(80 * zz, 16), 80)]

    for k in PEERS:
        send(chip_rows(z), chip_rows(z), p1v_s.at[k], p1v_r.at[k], dev(dz=k))
    got(dnp.at[oc], pair_s.at[1], pair_r.at[1])
    tdn[:, 0:80] = jnp.transpose(dnp[...].reshape(80, 128))
    dn1[z] = tdn[pl.ds(pl.multiple_of(32 * c, 32), 32), :].astype(BF16)
    for k in PEERS:
        send(dn1.at[z], dn1.at[z], p1d_s.at[k], p1d_r.at[k], dev(dz=k))

    loaded(0, 2, 14)
    signal = frames[...].astype(F32)
    center = signal - jnp.mean(signal, axis=1, keepdims=True)
    variance = jnp.mean(center * center, axis=1, keepdims=True)
    en = (center * lax.rsqrt(variance + EPSILON) * enc_gain[...].astype(F32).reshape(1, ENC)).astype(BF16)
    feature = lax.broadcasted_iota(jnp.int32, (ENC, 128), 0)
    for b in range(ENC // 128):
        cols = slice(128 * b, 128 * b + 128)
        pick = jnp.where(feature == source[:, cols], 1.0, 0.0).astype(BF16)
        en_p[c, :, cols] = nn(en, pick).astype(BF16)
    send(en_p.at[c], en_p.at[c], hp_s.at[0], hp_r.at[0], sibling)

    got(e1.at[y, oc], p1e_s.at[0, 1], p1e_r.at[0, 1])
    for k in PEERS:
        got(e1.at[(y + 8 - k) % Y, c], p1e_s.at[k, 0], p1e_r.at[k, 0])
        got(e1.at[(y + 8 - k) % Y, oc], p1e_s.at[k, 1], p1e_r.at[k, 1])
    for r in range(3):
        for yy in range(Y):
            for cc in range(2):
                et2[20 * yy + 10 * cc : 20 * yy + 10 * cc + 10, :] = e1[yy, cc, r].astype(F32)[0:10]
        E[e_index(r), z] = et2[...].astype(BF16)

    def e_part(s, d, way, r):
        return E.at[e_index(r), s] if d < 3 else E.at[e_index(r), s, pl.ds(80 * way, 80)]

    def e_send(way, d, r):
        s = (z + 8 - d) % Z if way == 0 else (z + d) % Z
        part = e_part(s, d, way, r)
        send(part, part, er_s.at[way, d, r], er_r.at[way, d, r], dev(dz=1 if way == 0 else 7))

    def e_across(s, n, r):
        if r < 2:
            send(E.at[e_index(r), s], E.at[e_index(r), s], ex_s.at[n, r], ex_r.at[n, r], dev(dx=1 if r == 0 else 3))

    def e_step(d, r):
        for way in range(2):
            s = (z + 7 - d) % Z if way == 0 else (z + 1 + d) % Z
            got(e_part(s, d, way, r), er_s.at[way, d, r], er_r.at[way, d, r])
            if d < 3:
                e_send(way, d + 1, r)
                e_across(s, 1 + 2 * d + way, r)
        if d == 3:
            e_across((z + 4) % Z, 7, r)

    for r in range(3):
        e_send(0, 0, r)
        e_send(1, 0, r)
        e_across(z, 0, r)

    e_step(0, 0)
    e_step(0, 1)

    for k in PEERS:
        got(chip_rows((z + 8 - k) % Z), p1v_s.at[k], p1v_r.at[k])

    def v_blk(s, i):
        return V.at[c, 2 * par + i, s]

    def x_blk(s, i):
        return V.at[c, 2 * (1 - par) + i, s]

    def v_send(way, d, i):
        s = (y + 8 - d) % Y if way == 0 else (y + d) % Y
        send(v_blk(s, i), v_blk(s, i), vy_s.at[way, d, i], vy_r.at[way, d, i], dev(dy=1 if way == 0 else 7))

    def v_spread(s, n, i):
        right = i == 0 if n in (0, 7) else i == (n + 1) % 2
        send(v_blk(s, i), v_blk(s, i), vx_s.at[i, n], vx_r.at[i, n], dev(dx=1 if right else 3))
        send(v_blk(s, i), v_blk(s, i), vd_s.at[n, i], vd_r.at[n, i], sibling)

    def v_step(d, i):
        for way in range(2):
            if d == 3 and way != i:
                continue
            s = (y + 7 - d) % Y if way == 0 else (y + 1 + d) % Y
            got(v_blk(s, i), vy_s.at[way, d, i], vy_r.at[way, d, i])
            if d < 2 or (d == 2 and way == i):
                v_send(way, d + 1, i)
            v_spread(s, 7 if d == 3 else 1 + 2 * d + way, i)

    def slab_of(n):
        d = (n + 1) // 2
        return (y + 8 - d) % Y if n % 2 == 1 else (y + d) % Y

    def x_step(n, i):
        s = slab_of(n)
        got(x_blk(s, i), vx_s.at[i, n], vx_r.at[i, n])
        send(x_blk(s, i), x_blk(s, i), vd_s.at[n, 2 + i], vd_r.at[n, 2 + i], sibling)

    def ready(n):
        s = slab_of(n)
        for i in range(2):
            got(V.at[oc, 2 * par + i, s], vd_s.at[n, i], vd_r.at[n, i])
            got(V.at[oc, 2 * (1 - par) + i, s], vd_s.at[n, 2 + i], vd_r.at[n, 2 + i])

    for i in range(2):
        v_send(0, 0, i)
        v_send(1, 0, i)
        v_spread(y, 0, i)

    e_step(0, 2)
    for k in PEERS:
        got(dn1.at[(z + 8 - k) % Z], p1d_s.at[k], p1d_r.at[k])
    DT[c, y] = jnp.concatenate([dn1[k].astype(F32)[:, 0:80] for k in range(Z)], axis=1).astype(BF16)

    def d_slab(s, d, way):
        return DT.at[c, s] if d < 3 else DT.at[c, s, pl.ds(16 * way, 16)]

    def d_send(d):
        send(d_slab((y + 8 - d) % Y, d, 0), d_slab((y + 8 - d) % Y, d, 0), dr_s.at[0, d], dr_r.at[0, d], dev(dy=1))
        send(d_slab((y + d) % Y, d, 1), d_slab((y + d) % Y, d, 1), dr_s.at[1, d], dr_r.at[1, d], dev(dy=7))

    def d_step(d):
        got(d_slab((y + 7 - d) % Y, d, 0), dr_s.at[0, d], dr_r.at[0, d])
        got(d_slab((y + 1 + d) % Y, d, 1), dr_s.at[1, d], dr_r.at[1, d])
        if d < 3:
            d_send(d + 1)

    d_send(0)

    loaded(13, 12, 11, 6, 5, 7, 1)
    cot[0:AUDIO_ROWS, :] = audio_cot[...]
    row = lax.broadcasted_iota(jnp.int32, (TEXT_ROWS, 1), 0)
    mask = jnp.where(row < live_text[...], 1.0, 0.0)
    cot[AUDIO_ROWS:ROWS, :] = (text_cot[...].astype(F32) * mask).astype(BF16)
    bl = (ADAPTER_SCALE * nt(cot[...], up[...])).astype(BF16)
    gains = [dec_gain[SLAB * k : SLAB * (k + 1)].astype(F32).reshape(1, SLAB) for k in range(Y)]
    square = jnp.zeros((TEXT_ROWS, 1), F32)
    for k in range(Y):
        part = text[:, SLAB * k : SLAB * (k + 1)].astype(F32)
        square += jnp.sum(part * part, axis=1, keepdims=True)
    inv_text = lax.rsqrt(square * (1.0 / DEC) + EPSILON)
    for k in range(Y):
        part = text[:, SLAB * k : SLAB * (k + 1)].astype(F32)
        xs[k, AUDIO_ROWS:ROWS, :] = part
        nrm[k, AUDIO_ROWS:ROWS, :] = (part * inv_text * gains[k]).astype(BF16)

    def whole(s):
        return jnp.concatenate([V[b // 4, b % 4, s] for b in range(8)], axis=1)

    def backward(n):
        s = slab_of(n)
        gn[s] = nt(cot[...], whole(s))

    def forward(n):
        s = slab_of(n)
        product = nn(nrm[s], whole(s))
        acc[...] = product if n == 0 else acc[...] + product

    e_step(1, 0)
    e_step(1, 1)
    e_step(1, 2)
    d_step(0)
    e_step(2, 0)
    v_step(0, 0)
    e_step(2, 1)
    x_step(0, 0)
    x_step(0, 1)
    e_step(2, 2)
    d_step(1)
    e_step(3, 0)
    e_step(3, 1)
    e_step(3, 2)
    v_step(0, 1)
    d_step(2)

    for n in range(8):
        d = (n + 1) // 2
        s = (z + 8 - d) % Z if n % 2 == 1 else (z + d) % Z
        for r in range(2):
            got(E.at[3 * (1 - par) + r, s], ex_s.at[n, r], ex_r.at[n, r])
    got(en_p.at[oc], hp_s.at[0], hp_r.at[0])
    mine = jnp.concatenate([E[b].reshape(ENC, 128) for b in range(5)], axis=1)
    hbuf[...] = nn(en_p[...].reshape(8 * AUDIO_ROWS, ENC), mine).reshape(2, 4 * AUDIO_ROWS, HALF)
    send(hbuf.at[oc], hall.at[c], hp_s.at[1], hp_r.at[1], sibling)
    hall[c] = hbuf[c]
    x_step(1, 0)
    x_step(2, 0)
    v_step(1, 0)
    got(hall.at[oc], hp_s.at[1], hp_r.at[1])
    frame = lax.broadcasted_iota(jnp.int32, (4 * AUDIO_ROWS, 1), 0)
    live = jnp.where(frame < live_frames[...], 1.0, 0.0)
    for h in range(2):
        cols = slice(HALF * h, HALF * (h + 1))
        hidden = hall[h]
        gelu = 0.5 * hidden * (1.0 + erf(hidden * (1.0 / math.sqrt(2.0))))
        encoded = ((frames[:, cols].astype(F32) + gelu) * live).astype(BF16)
        for b in range(5):
            enc_f[5 * h + b] = encoded[:, 128 * b : 128 * b + 128].astype(F32)
    square = jnp.zeros((AUDIO_ROWS, 1), F32)
    for k in range(4):
        for b in range(10):
            part = enc_f[b, pl.ds(k, AUDIO_ROWS, stride=4), :]
            square += jnp.sum(part * part, axis=1, keepdims=True)
            xs[2 * k + b // 5, 0:AUDIO_ROWS, 128 * (b % 5) : 128 * (b % 5) + 128] = part
    inv_audio = lax.rsqrt(square * (1.0 / DEC) + EPSILON)
    for k in range(Y):
        nrm[k, 0:AUDIO_ROWS, :] = (xs[k, 0:AUDIO_ROWS, :] * inv_audio * gains[k]).astype(BF16)

    d_step(3)
    send(DT.at[c], DT.at[c], dd_s.at[0], dd_r.at[0], sibling)
    v_step(1, 1)
    x_step(1, 1)
    x_step(2, 1)
    got(DT.at[oc], dd_s.at[0], dd_r.at[0])
    low = jnp.zeros((ROWS, RANK), F32)
    for k in range(Y):
        low += nt(nrm[k], jnp.concatenate([DT[0, k], DT[1, k]], axis=0))
    lr = low.astype(BF16)
    twice = one_hot(RANK, 128, lambda i, j: (j == i) | (j == i + RANK))
    bl2 = nn(bl, twice).astype(BF16)
    lr2 = nn(lr, twice).astype(BF16)
    first = lax.broadcasted_iota(jnp.int32, (24, 128), 1) < RANK
    g_up = tn(cot[...], lr2) * (ADAPTER_SCALE * MULTIPLIER)
    for k in range(Y):
        g_down = tn(nrm[k], bl2) * MULTIPLIER
        for zz in range(Z):
            for cc in range(2):
                at = 80 * zz + 40 * cc
                u = 16 * (Z * k + zz) + 8 * cc
                tail = jnp.concatenate([g_down[at + 24 : at + 40], g_up[u : u + 8]], axis=0)
                R1[cc, zz, 24 * k : 24 * k + 24, :] = jnp.where(first, g_down[at : at + 24], tail)
    send(R1.at[oc], R2, rp_s.at[0], rp_r.at[0], sibling)

    x_step(3, 0)
    x_step(4, 0)
    v_step(2, 0)
    got(R2, rp_s.at[0], rp_r.at[0])
    for k in PEERS:
        at = (z + k) % Z
        RZs[at] = (R1[c, at] + R2[at]).astype(BF16)
        send(RZs.at[at], RZr.at[k], rz_s.at[k], rz_r.at[k], dev(dz=k))
    for n in range(3):
        ready(n)
        backward(n)
        forward(n)
    v_step(2, 1)
    x_step(3, 1)
    x_step(4, 1)
    v_step(3, 0)
    v_step(3, 1)
    x_step(5, 0)
    x_step(6, 0)
    for n in range(3, 5):
        ready(n)
        backward(n)
        forward(n)
    x_step(5, 1)
    x_step(6, 1)

    total = R1[c, z] + R2[z]
    for k in PEERS:
        got(RZr.at[k], rz_s.at[k], rz_r.at[k])
        total += RZr[k].astype(F32)
    for yy in range(Y):
        RYs[yy] = total[24 * yy : 24 * yy + 24]
    for k in PEERS:
        send(RYs.at[(y + k) % Y], RYr.at[k], ry_s.at[k], ry_r.at[k], dev(dy=k))

    for n in range(5, 7):
        ready(n)
        backward(n)
        forward(n)
    x_step(7, 0)
    x_step(7, 1)
    ready(7)
    backward(7)
    forward(7)
    values = (acc[...] + ADAPTER_SCALE * nn(lr, up[...])).astype(BF16)
    out_av[...] = values[0:AUDIO_ROWS]
    out_tv[...] = values[AUDIO_ROWS:ROWS]
    inverse = jnp.concatenate([inv_audio, inv_text], axis=0)
    mean = jnp.zeros((ROWS, 1), F32)
    for k in range(Y):
        both = jnp.concatenate([DT[0, k], DT[1, k]], axis=0)
        u = (gn[k] + nn(bl, both)) * gains[k]
        gn[k] = u
        mean += jnp.sum(u * xs[k], axis=1, keepdims=True)

    total = RYs[y]
    for k in PEERS:
        got(RYr.at[k], ry_s.at[k], ry_r.at[k])
        total += RYr[k]
    FX[x] = total
    for k in range(1, X):
        send(FX.at[x], FX.at[x], rx_s.at[k], rx_r.at[k], dev(dx=k))

    scale = inverse * inverse * inverse * (mean * (1.0 / DEC))
    for k in range(Y):
        cols = slice(SLAB * k, SLAB * (k + 1))
        grad = (inverse * gn[k] - xs[k] * scale).astype(BF16)
        out_ag[:, cols] = grad[0:AUDIO_ROWS]
        out_tg[:, cols] = grad[AUDIO_ROWS:ROWS]

    for k in range(1, X):
        got(FX.at[(x + 4 - k) % X], rx_s.at[k], rx_r.at[k])
    total = FX[0] + FX[1] + FX[2] + FX[3]
    right = pltpu.roll(total, RANK, axis=1)
    out_gd[0:24, :] = total[:, :RANK]
    out_gd[24:40, :] = right[0:16, :RANK]
    out_gu[...] = right[16:24, :RANK]

    for copy in sent:
        copy.wait_send()


def hand_over(*refs):
    given, out, held, sems = refs[:6], refs[6:12], refs[12:18], refs[18]
    order = (3, 2, 1, 0, 4, 5)
    loads = [pltpu.make_async_copy(given[i], held[i], sems.at[0, i]) for i in range(6)]
    stores = [pltpu.make_async_copy(held[i], out[i], sems.at[1, i]) for i in range(6)]
    for i in order:
        loads[i].start()
    for i in order:
        loads[i].wait()
        stores[i].start()
    for i in order:
        stores[i].wait()


def natural_features():
    place = np.arange(ENC)
    return (160 * (place % 160 // 20) + 20 * (place // 160) + place % 20).astype(np.int32)[None]


def shards(
    frames, live_frames, enc_gain, enc_q, enc_s, text, live_text, dec_gain, val_q, val_s,
    down, up, audio_cot, text_cot,
):
    operands = (
        frames,
        live_frames.reshape(1, 1),
        enc_gain,
        enc_q,
        enc_s,
        text,
        live_text.reshape(1, 1),
        dec_gain,
        val_q,
        val_s.T,
        down,
        up.T,
        audio_cot,
        text_cot,
        jnp.asarray(natural_features()),
    )
    dma = pltpu.SemaphoreType.DMA
    vmem = pltpu.VMEM
    results = pl.pallas_call(
        kernel,
        out_shape=(
            jax.ShapeDtypeStruct((AUDIO_ROWS, VALUE), BF16),
            jax.ShapeDtypeStruct((TEXT_ROWS, VALUE), BF16),
            jax.ShapeDtypeStruct((AUDIO_ROWS, DEC), BF16),
            jax.ShapeDtypeStruct((TEXT_ROWS, DEC), BF16),
            jax.ShapeDtypeStruct((40, RANK), F32),
            jax.ShapeDtypeStruct((8, RANK), F32),
        ),
        in_specs=[pl.BlockSpec(memory_space=pltpu.HBM)] * 15,
        out_specs=[pl.BlockSpec(memory_space=vmem)] * 6,
        scratch_shapes=[
            *(vmem(a.shape, a.dtype) for a in operands),
            vmem((2, 4, Y, SLAB, 128), BF16),
            vmem((5, Z, 160, 128), BF16),
            vmem((2, Y, 32, SLAB), BF16),
            vmem((Y, 2, 3, 16, 128), BF16),
            vmem((2, 40, 128), F32),
            vmem((128, 128), F32),
            vmem((Z, 32, 128), BF16),
            vmem((2, 5, 16, 128), BF16),
            vmem((2, 3, 16, 128), BF16),
            vmem((16, ENC), F32),
            vmem((160, 128), F32),
            vmem((2, 4, 40, 128), F32),
            vmem((2, 2, 40, 128), F32),
            vmem((ROWS, VALUE), BF16),
            vmem((Y, ROWS, SLAB), F32),
            vmem((Y, ROWS, SLAB), BF16),
            vmem((Y, ROWS, SLAB), F32),
            vmem((ROWS, VALUE), F32),
            vmem((ENC // 128, 4 * AUDIO_ROWS, 128), F32),
            vmem((2, 4 * AUDIO_ROWS, ENC), BF16),
            vmem((2, 4 * AUDIO_ROWS, HALF), F32),
            vmem((2, 4 * AUDIO_ROWS, HALF), F32),
            vmem((2, Z, 24 * Y, 128), F32),
            vmem((Z, 24 * Y, 128), F32),
            vmem((Z, 24 * Y, 128), BF16),
            vmem((Z, 24 * Y, 128), BF16),
            vmem((Y, 24, 128), F32),
            vmem((Y, 24, 128), F32),
            vmem((X, 24, 128), F32),
        ]
        + [dma((15,))]
        + [
            dma(shape)
            for shape in (
                (2,), (8,), (8, 2), (8,), (2, 4, 3), (8, 2), (2,), (2, 4), (1,), (2, 4, 2), (2, 8), (8, 4),
                (1,), (8,), (8,), (4,),
            )
            for _ in range(2)
        ],
        compiler_params=pltpu.CompilerParams(
            collective_id=0, has_side_effects=True, vmem_limit_bytes=60 * 1024 * 1024
        ),
        cost_estimate=pl.CostEstimate(
            flops=2 * ROWS * (2 * DEC * VALUE + ENC * ENC), bytes_accessed=6_000_000, transcendentals=0
        ),
    )(*operands)
    return pl.pallas_call(
        hand_over,
        out_shape=tuple(jax.ShapeDtypeStruct(a.shape, a.dtype) for a in results),
        in_specs=[pl.BlockSpec(memory_space=pl.ANY)] * 6,
        out_specs=[pl.BlockSpec(memory_space=pl.ANY)] * 6,
        scratch_shapes=[*(vmem(a.shape, a.dtype) for a in results), dma((2, 6))],
        compiler_params=pltpu.CompilerParams(vmem_limit_bytes=60 * 1024 * 1024),
    )(*results)


def solution(mesh):
    both = ("dp", "fsdp")
    in_specs = (
        P(both, None), P(both), P(), P("fsdp", None), P("fsdp", None), P(both, None), P(both), P(),
        P("fsdp", None), P("fsdp", None), P("fsdp", None), P(), P(both, None), P(both, None),
    )
    out_specs = (
        P(both, None), P(both, None), P(both, None), P(both, None), P("fsdp", None), P("fsdp", None),
    )
    return jax.shard_map(shards, mesh=mesh, in_specs=in_specs, out_specs=out_specs, check_vma=False)
```

```python
import math

import jax
import jax.numpy as jnp
import numpy as np
from jax import lax
from jax.experimental import pallas as pl
from jax.experimental.pallas import tpu as pltpu
from jax.sharding import PartitionSpec as P

MESH = pl.DeviceIdType.MESH
F32 = jnp.float32
BF16 = jnp.bfloat16

EPSILON = 1e-05
ADAPTER_SCALE = 2.0
X, Y, Z = 4, 8, 8
AUDIO_ROWS, TEXT_ROWS = 32, 96
ROWS = AUDIO_ROWS + TEXT_ROWS
ENC = 1280
HALF = ENC // 2
DEC = 5120
SLAB = DEC // Y
VALUE = 1024
RANK = 64
MULTIPLIER = 1.0 / math.sqrt(X * Y * Z * 2 * ROWS)

PEERS = (1, 7, 2, 6, 3, 5, 4)


ORDER = (
    "perm", "Pe", "e00", "Pd", "Pv", "e01", "e02", "rows", "e10", "d0", "e11", "e12",
    "v00", "e20", "e21", "e22", "d1", "e30", "e31", "e32", "v01", "d2", "x00", "x01",
    "hid", "x10", "x20", "v10", "enc", "gd", "d3", "share", "v11", "za", "x11", "x21",
    "gu", "v20", "zb", "x30", "x40", "b0", "f0", "v21", "x31", "x41", "b1", "f1",
    "b2", "f2", "x50", "x60", "v30", "v31", "b3", "f3", "b4", "f4", "ya", "x51",
    "x61", "b5", "f5", "b6", "f6", "rx", "x70", "x71", "b7", "f7", "vals", "out",
    "fin",
)


def nn(a, b):
    return lax.dot_general(a, b, (((1,), (0,)), ((), ())), preferred_element_type=F32)


def nt(a, b):
    return lax.dot_general(a, b, (((1,), (1,)), ((), ())), preferred_element_type=F32)


def tn(a, b):
    return lax.dot_general(a, b, (((0,), (0,)), ((), ())), preferred_element_type=F32)


def one_hot(rows, columns, hit):
    i = lax.broadcasted_iota(jnp.int32, (rows, columns), 0)
    j = lax.broadcasted_iota(jnp.int32, (rows, columns), 1)
    return jnp.where(hit(i, j), 1.0, 0.0).astype(BF16)


def spread(blocks):
    return one_hot(blocks, blocks * 64, lambda i, j: (j >= 64 * i) & (j < 64 * i + 64))


def erf(x):
    x = jnp.clip(x, -3.832506856900711, 3.832506856900711)
    s = x * x
    p = jnp.full_like(s, 0.00022905065861350646)
    for k in (0.0034082910107109506, 0.050955695062380861, 0.18520832239976145, 1.128379143519084):
        p = p * s + k
    q = jnp.full_like(s, -1.1791602954361697e-7)
    for k in (
        0.000023547966471313185,
        0.0010179625278914885,
        0.014070470171167667,
        0.11098505178285362,
        0.49746925110067538,
        1.0,
    ):
        q = q * s + k
    return x * p / q


def kernel(
    *refs,
):
    given, refs = refs[:15], refs[15:]
    out_av, out_tv, out_ag, out_tg, out_gd, out_gu = refs[:6]
    held, refs = refs[6:21], refs[21:]
    (
        frames, live_frames, enc_gain, enc_q, enc_s, text, live_text, dec_gain, val_q, val_s,
        down, up, audio_cot, text_cot, source,
    ) = held
    (
    V, E, DT, e1, dnp, tdn, dn1, ebuf, emine, et, et2, wv, vx, cot, xs, nrm, gn, acc, enc_f, en_p,
    hall, hbuf, gain_rows,
    RA, RA2, RAs, RAr, TA, TAr, RB, RB2, RBs, RBr, FX,
    in_sem, pair_s, pair_r, p1v_s, p1v_r, p1e_s, p1e_r, p1d_s, p1d_r,
    er_s, er_r, ex_s, ex_r, hp_s, hp_r, dr_s, dr_r, dd_s, dd_r, vy_s, vy_r, vx_s, vx_r, vd_s, vd_r,
    rp_s, rp_r, za_s, za_r, zb_s, zb_r, ya_s, ya_r, rx_s, rx_r,
    ) = refs
    x = lax.axis_index("dp")
    f = lax.axis_index("fsdp")
    c = f % 2
    z = (f // 2) % Z
    y = f // (2 * Z)
    par = x % 2
    oc = 1 - c

    def dev(dx=0, dy=0, dz=0, core=None):
        return (
            (x + dx) % X if dx else x,
            (((y + dy) % Y if dy else y) * Z + ((z + dz) % Z if dz else z)) * 2
            + (c if core is None else core),
        )

    sibling = dev(core=oc)
    sent = []

    def send(src, dst, ss, rs, to):
        copy = pltpu.make_async_remote_copy(
            src_ref=src, dst_ref=dst, send_sem=ss, recv_sem=rs, device_id=to, device_id_type=MESH
        )
        copy.start()
        sent.append(copy)

    def got(dst, ss, rs):
        pltpu.make_async_remote_copy(
            src_ref=dst, dst_ref=dst, send_sem=ss, recv_sem=rs, device_id=sibling,
            device_id_type=MESH,
        ).wait_recv()

    barrier = pltpu.get_barrier_semaphore()
    peers = [sibling]
    peers += [dev(dx=k) for k in range(1, X)]
    peers += [dev(dy=k, core=core) for k in range(1, Y) for core in (c, oc)]
    peers += [dev(dz=k) for k in range(1, Z)]
    for peer in peers:
        pl.semaphore_signal(barrier, inc=1, device_id=peer, device_id_type=MESH)

    loads = [pltpu.make_async_copy(given[i], held[i], in_sem.at[i]) for i in range(15)]
    for i in (4, 3, 10, 9, 8, 0, 2, 14, 13, 12, 11, 6, 5, 7, 1):
        loads[i].start()

    def loaded(*indices):
        for i in indices:
            loads[i].wait()

    def e_index(r):
        return 2 if r == 2 else 3 * par + r

    et[...] = jnp.zeros_like(et)
    loaded(4, 3)
    et[0:10, :] = enc_q[...].astype(F32) * nn(enc_s[...], spread(ENC // 64))
    for b in range(10):
        ebuf[b // 5, b % 5] = et[:, 128 * b : 128 * b + 128].astype(BF16)
    for h in range(2):
        for r in range(3):
            emine[h, r] = ebuf[h, e_index(r)]
    e1[y, c] = emine[c]

    pl.semaphore_wait(barrier, len(peers))

    send(emine.at[oc], e1.at[y, c], p1e_s.at[0, 1], p1e_r.at[0, 1], sibling)
    for k in PEERS:
        send(emine.at[c], e1.at[y, c], p1e_s.at[k, 0], p1e_r.at[k, 0], dev(dy=k))
        send(emine.at[oc], e1.at[y, c], p1e_s.at[k, 1], p1e_r.at[k, 1], dev(dy=k, core=oc))
    loaded(10)
    dnp[c] = nn(down[...], one_hot(RANK, 128, lambda i, j: i == j))
    tdn[...] = jnp.zeros_like(tdn)
    send(dnp.at[c], dnp.at[c], pair_s.at[1], pair_r.at[1], sibling)
    loaded(9, 8)
    weight = val_q[...].astype(F32) * tn(val_s[...], spread(VALUE // 64))
    for b in range(8):
        wv[b // 4, b % 4] = weight[:, 128 * b : 128 * b + 128]
    vx[c] = wv[c, pl.ds(2 * par, 2)]
    send(wv.at[oc, pl.ds(2 * par, 2)], vx.at[c], pair_s.at[0], pair_r.at[0], sibling)

    got(dnp.at[oc], pair_s.at[1], pair_r.at[1])
    tdn[:, 0:80] = jnp.transpose(dnp[...].reshape(80, 128))
    dn1[z] = tdn[pl.ds(pl.multiple_of(32 * c, 32), 32), :].astype(BF16)
    for k in PEERS:
        send(dn1.at[z], dn1.at[z], p1d_s.at[k], p1d_r.at[k], dev(dz=k))
    got(vx.at[oc], pair_s.at[0], pair_r.at[0])
    for i in range(2):
        V[c, 2 * par + i, y, pl.ds(pl.multiple_of(80 * z, 16), 80), :] = jnp.concatenate(
            [vx[0, i], vx[1, i]], axis=0
        ).astype(BF16)

    def chip_rows(zz):
        return V.at[c, pl.ds(2 * par, 2), y, pl.ds(pl.multiple_of(80 * zz, 16), 80)]

    for k in PEERS:
        send(chip_rows(z), chip_rows(z), p1v_s.at[k], p1v_r.at[k], dev(dz=k))

    def e_part(s, d, way, r):
        return E.at[e_index(r), s] if d < 3 else E.at[e_index(r), s, pl.ds(80 * way, 80)]

    def e_send(way, d, r):
        s = (z + 8 - d) % Z if way == 0 else (z + d) % Z
        part = e_part(s, d, way, r)
        send(part, part, er_s.at[way, d, r], er_r.at[way, d, r], dev(dz=1 if way == 0 else 7))

    def e_across(s, n, r):
        if r < 2:
            send(E.at[e_index(r), s], E.at[e_index(r), s], ex_s.at[n, r], ex_r.at[n, r], dev(dx=1 if r == 0 else 3))

    def e_step(d, r):
        for way in range(2):
            s = (z + 7 - d) % Z if way == 0 else (z + 1 + d) % Z
            got(e_part(s, d, way, r), er_s.at[way, d, r], er_r.at[way, d, r])
            if d < 3:
                e_send(way, d + 1, r)
                e_across(s, 1 + 2 * d + way, r)
        if d == 3:
            e_across((z + 4) % Z, 7, r)

    def v_blk(s, i):
        return V.at[c, 2 * par + i, s]

    def x_blk(s, i):
        return V.at[c, 2 * (1 - par) + i, s]

    def v_send(way, d, i):
        s = (y + 8 - d) % Y if way == 0 else (y + d) % Y
        send(v_blk(s, i), v_blk(s, i), vy_s.at[way, d, i], vy_r.at[way, d, i], dev(dy=1 if way == 0 else 7))

    def v_spread(s, n, i):
        right = i == 0 if n in (0, 7) else i == (n + 1) % 2
        send(v_blk(s, i), v_blk(s, i), vx_s.at[i, n], vx_r.at[i, n], dev(dx=1 if right else 3))
        send(v_blk(s, i), v_blk(s, i), vd_s.at[n, i], vd_r.at[n, i], sibling)

    def v_step(d, i):
        for way in range(2):
            if d == 3 and way != i:
                continue
            s = (y + 7 - d) % Y if way == 0 else (y + 1 + d) % Y
            got(v_blk(s, i), vy_s.at[way, d, i], vy_r.at[way, d, i])
            if d < 2 or (d == 2 and way == i):
                v_send(way, d + 1, i)
            v_spread(s, 7 if d == 3 else 1 + 2 * d + way, i)

    def slab_of(n):
        d = (n + 1) // 2
        return (y + 8 - d) % Y if n % 2 == 1 else (y + d) % Y

    def x_step(n, i):
        s = slab_of(n)
        got(x_blk(s, i), vx_s.at[i, n], vx_r.at[i, n])
        send(x_blk(s, i), x_blk(s, i), vd_s.at[n, 2 + i], vd_r.at[n, 2 + i], sibling)

    def ready(n):
        s = slab_of(n)
        for i in range(2):
            got(V.at[oc, 2 * par + i, s], vd_s.at[n, i], vd_r.at[n, i])
            got(V.at[oc, 2 * (1 - par) + i, s], vd_s.at[n, 2 + i], vd_r.at[n, 2 + i])

    def d_slab(s, d, way):
        return DT.at[c, s] if d < 3 else DT.at[c, s, pl.ds(16 * way, 16)]

    def d_send(d):
        send(d_slab((y + 8 - d) % Y, d, 0), d_slab((y + 8 - d) % Y, d, 0), dr_s.at[0, d], dr_r.at[0, d], dev(dy=1))
        send(d_slab((y + d) % Y, d, 1), d_slab((y + d) % Y, d, 1), dr_s.at[1, d], dr_r.at[1, d], dev(dy=7))

    def d_step(d):
        got(d_slab((y + 7 - d) % Y, d, 0), dr_s.at[0, d], dr_r.at[0, d])
        got(d_slab((y + 1 + d) % Y, d, 1), dr_s.at[1, d], dr_r.at[1, d])
        if d < 3:
            d_send(d + 1)

    state = {}

    def whole(s):
        return jnp.concatenate([V[b // 4, b % 4, s] for b in range(8)], axis=1)

    def backward(n):
        s = slab_of(n)
        gn[s] = nt(cot[...], whole(s))

    def forward(n):
        s = slab_of(n)
        product = nn(nrm[s], whole(s))
        acc[...] = product if n == 0 else acc[...] + product
        adapter = nn(state["bl"], jnp.concatenate([DT[0, s], DT[1, s]], axis=0))
        u = (gn[s] + adapter) * gain_rows[s]
        gn[s] = u
        part = jnp.sum(u * xs[s], axis=1, keepdims=True)
        state["mean"] = part if n == 0 else state["mean"] + part


    def twice():
        return one_hot(RANK, 128, lambda i, j: (j == i) | (j == i + RANK))

    def first(height):
        return lax.broadcasted_iota(jnp.int32, (height, 128), 1) < RANK

    def share_d():
        send(DT.at[c], DT.at[c], dd_s.at[0], dd_r.at[0], sibling)

    def do_start_e():
        got(e1.at[y, oc], p1e_s.at[0, 1], p1e_r.at[0, 1])
        for k in PEERS:
            got(e1.at[(y + 8 - k) % Y, c], p1e_s.at[k, 0], p1e_r.at[k, 0])
            got(e1.at[(y + 8 - k) % Y, oc], p1e_s.at[k, 1], p1e_r.at[k, 1])
        for r in range(3):
            for yy in range(Y):
                for cc in range(2):
                    et2[20 * yy + 10 * cc : 20 * yy + 10 * cc + 10, :] = e1[yy, cc, r].astype(F32)[0:10]
            E[e_index(r), z] = et2[...].astype(BF16)

        for r in range(3):
            e_send(0, 0, r)
            e_send(1, 0, r)
            e_across(z, 0, r)

    def do_start_v():
        for k in PEERS:
            got(chip_rows((z + 8 - k) % Z), p1v_s.at[k], p1v_r.at[k])

        for i in range(2):
            v_send(0, 0, i)
            v_send(1, 0, i)
            v_spread(y, 0, i)

    def do_start_d():
        for k in PEERS:
            got(dn1.at[(z + 8 - k) % Z], p1d_s.at[k], p1d_r.at[k])
        DT[c, y] = jnp.concatenate([dn1[k].astype(F32)[:, 0:80] for k in range(Z)], axis=1).astype(BF16)

        d_send(0)

    def do_perm():
        loaded(0, 2, 14)
        signal = frames[...].astype(F32)
        center = signal - jnp.mean(signal, axis=1, keepdims=True)
        variance = jnp.mean(center * center, axis=1, keepdims=True)
        en = (center * lax.rsqrt(variance + EPSILON) * enc_gain[...].astype(F32).reshape(1, ENC)).astype(BF16)
        feature = lax.broadcasted_iota(jnp.int32, (ENC, 128), 0)
        for b in range(ENC // 128):
            cols = slice(128 * b, 128 * b + 128)
            pick = jnp.where(feature == source[:, cols], 1.0, 0.0).astype(BF16)
            en_p[c, :, cols] = nn(en, pick).astype(BF16)
        send(en_p.at[c], en_p.at[c], hp_s.at[0], hp_r.at[0], sibling)

    def do_rows():
        loaded(13, 12, 11, 6, 5, 7, 1)
        cot[0:AUDIO_ROWS, :] = audio_cot[...]
        row = lax.broadcasted_iota(jnp.int32, (TEXT_ROWS, 1), 0)
        mask = jnp.where(row < live_text[...], 1.0, 0.0)
        cot[AUDIO_ROWS:ROWS, :] = (text_cot[...].astype(F32) * mask).astype(BF16)
        state["bl"] = (ADAPTER_SCALE * nt(cot[...], up[...])).astype(BF16)
        gains = [dec_gain[SLAB * k : SLAB * (k + 1)].astype(F32).reshape(1, SLAB) for k in range(Y)]
        for k in range(Y):
            gain_rows[k] = gains[k]
        square = jnp.zeros((TEXT_ROWS, 1), F32)
        for k in range(Y):
            part = text[:, SLAB * k : SLAB * (k + 1)].astype(F32)
            square += jnp.sum(part * part, axis=1, keepdims=True)
        state["inv_text"] = inv_text = lax.rsqrt(square * (1.0 / DEC) + EPSILON)
        for k in range(Y):
            part = text[:, SLAB * k : SLAB * (k + 1)].astype(F32)
            xs[k, AUDIO_ROWS:ROWS, :] = part
            nrm[k, AUDIO_ROWS:ROWS, :] = (part * inv_text * gains[k]).astype(BF16)

    def do_hid():
        for n in range(8):
            d = (n + 1) // 2
            s = (z + 8 - d) % Z if n % 2 == 1 else (z + d) % Z
            for r in range(2):
                got(E.at[3 * (1 - par) + r, s], ex_s.at[n, r], ex_r.at[n, r])
        got(en_p.at[oc], hp_s.at[0], hp_r.at[0])
        mine = jnp.concatenate([E[b].reshape(ENC, 128) for b in range(5)], axis=1)
        hbuf[...] = nn(en_p[...].reshape(8 * AUDIO_ROWS, ENC), mine).reshape(2, 4 * AUDIO_ROWS, HALF)
        send(hbuf.at[oc], hall.at[c], hp_s.at[1], hp_r.at[1], sibling)
        hall[c] = hbuf[c]

    def do_enc():
        got(hall.at[oc], hp_s.at[1], hp_r.at[1])
        frame = lax.broadcasted_iota(jnp.int32, (4 * AUDIO_ROWS, 1), 0)
        live = jnp.where(frame < live_frames[...], 1.0, 0.0)
        for h in range(2):
            cols = slice(HALF * h, HALF * (h + 1))
            hidden = hall[h]
            gelu = 0.5 * hidden * (1.0 + erf(hidden * (1.0 / math.sqrt(2.0))))
            encoded = ((frames[:, cols].astype(F32) + gelu) * live).astype(BF16)
            for b in range(5):
                enc_f[5 * h + b] = encoded[:, 128 * b : 128 * b + 128].astype(F32)
        square = jnp.zeros((AUDIO_ROWS, 1), F32)
        for k in range(4):
            for b in range(10):
                part = enc_f[b, pl.ds(k, AUDIO_ROWS, stride=4), :]
                square += jnp.sum(part * part, axis=1, keepdims=True)
                xs[2 * k + b // 5, 0:AUDIO_ROWS, 128 * (b % 5) : 128 * (b % 5) + 128] = part
        state["inv_audio"] = inv_audio = lax.rsqrt(square * (1.0 / DEC) + EPSILON)
        for k in range(Y):
            nrm[k, 0:AUDIO_ROWS, :] = (xs[k, 0:AUDIO_ROWS, :] * inv_audio * gain_rows[k]).astype(BF16)

    def do_gd():
        bl2 = nn(state["bl"], twice()).astype(BF16)
        for k in range(Y):
            g_down = tn(nrm[k], bl2) * MULTIPLIER
            for zz in range(Z):
                for cc in range(2):
                    at = 80 * zz + 40 * cc
                    RA[cc, zz, 16 * k : 16 * k + 16, :] = jnp.where(
                        first(16), g_down[at : at + 16], g_down[at + 24 : at + 40]
                    )
                    RB[cc, zz, 8 * k : 8 * k + 8, :] = g_down[at + 16 : at + 24]
        send(RA.at[oc], RA2, rp_s.at[0], rp_r.at[0], sibling)

    def do_gu():
        got(DT.at[oc], dd_s.at[0], dd_r.at[0])
        low = jnp.zeros((ROWS, RANK), F32)
        for k in range(Y):
            low += nt(nrm[k], jnp.concatenate([DT[0, k], DT[1, k]], axis=0))
        state["lr"] = lr = low.astype(BF16)
        lr2 = nn(lr, twice()).astype(BF16)
        g_up = tn(cot[...], lr2) * (ADAPTER_SCALE * MULTIPLIER)
        for k in range(Y):
            for zz in range(Z):
                for cc in range(2):
                    u = 16 * (Z * k + zz) + 8 * cc
                    part = RB[cc, zz, 8 * k : 8 * k + 8, :]
                    RB[cc, zz, 8 * k : 8 * k + 8, :] = jnp.where(first(8), part, g_up[u : u + 8])
        send(RB.at[oc], RB2, rp_s.at[1], rp_r.at[1], sibling)

    def do_za():
        got(RA2, rp_s.at[0], rp_r.at[0])
        for k in PEERS:
            at = (z + k) % Z
            RAs[at] = (RA[c, at] + RA2[at]).astype(BF16)
            send(RAs.at[at], RAr.at[k], za_s.at[k], za_r.at[k], dev(dz=k))

    def do_zb():
        got(RB2, rp_s.at[1], rp_r.at[1])
        for k in PEERS:
            at = (z + k) % Z
            RBs[at] = (RB[c, at] + RB2[at]).astype(BF16)
            send(RBs.at[at], RBr.at[k], zb_s.at[k], zb_r.at[k], dev(dz=k))

    def do_ya():
        part_a, part_b = RA[c, z] + RA2[z], RB[c, z] + RB2[z]
        for k in PEERS:
            got(RAr.at[k], za_s.at[k], za_r.at[k])
            part_a += RAr[k].astype(F32)
        for k in PEERS:
            got(RBr.at[k], zb_s.at[k], zb_r.at[k])
            part_b += RBr[k].astype(F32)
        for yy in range(Y):
            TA[yy, 0:16, :] = part_a[16 * yy : 16 * yy + 16]
            TA[yy, 16:24, :] = part_b[8 * yy : 8 * yy + 8]
        for k in PEERS:
            send(TA.at[(y + k) % Y], TAr.at[k], ya_s.at[k], ya_r.at[k], dev(dy=k))

    def do_rx():
        total = TA[y]
        for k in PEERS:
            got(TAr.at[k], ya_s.at[k], ya_r.at[k])
            total += TAr[k]
        FX[x] = total
        for k in range(1, X):
            send(FX.at[x], FX.at[x], rx_s.at[k], rx_r.at[k], dev(dx=k))

    def do_vals():
        values = (acc[...] + ADAPTER_SCALE * nn(state["lr"], up[...])).astype(BF16)
        out_av[...] = values[0:AUDIO_ROWS]
        out_tv[...] = values[AUDIO_ROWS:ROWS]
        inverse = jnp.concatenate([state["inv_audio"], state["inv_text"]], axis=0)
        state["inverse"] = inverse

    def do_out():
        inverse, mean = state["inverse"], state["mean"]
        scale = inverse * inverse * inverse * (mean * (1.0 / DEC))
        for k in range(Y):
            cols = slice(SLAB * k, SLAB * (k + 1))
            grad = (inverse * gn[k] - xs[k] * scale).astype(BF16)
            out_ag[:, cols] = grad[0:AUDIO_ROWS]
            out_tg[:, cols] = grad[AUDIO_ROWS:ROWS]

    def do_fin():
        for k in range(1, X):
            got(FX.at[(x + 4 - k) % X], rx_s.at[k], rx_r.at[k])
        total = FX[0] + FX[1] + FX[2] + FX[3]
        right = pltpu.roll(total, RANK, axis=1)
        out_gd[0:24, :] = total[:, :RANK]
        out_gd[24:40, :] = right[0:16, :RANK]
        out_gu[...] = right[16:24, :RANK]

    def slab(n):
        ready(n)
        backward(n)

    named = {
        "Pe": do_start_e, "Pv": do_start_v, "Pd": do_start_d, "perm": do_perm, "rows": do_rows, "hid": do_hid,
        "enc": do_enc, "gd": do_gd, "gu": do_gu, "za": do_za, "zb": do_zb, "ya": do_ya, "rx": do_rx, "vals": do_vals, "out": do_out,
        "fin": do_fin, "share": share_d,
    }
    steps = {"e": e_step, "d": d_step, "v": v_step, "x": x_step, "b": slab, "f": forward}
    for step in ORDER:
        if step in named:
            named[step]()
        else:
            steps[step[0]](*(int(digit) for digit in step[1:]))

    for copy in sent:
        copy.wait_send()


def hand_over(*refs):
    given, out, held, sems = refs[:6], refs[6:12], refs[12:18], refs[18]
    order = (3, 2, 1, 0, 4, 5)
    loads = [pltpu.make_async_copy(given[i], held[i], sems.at[0, i]) for i in range(6)]
    stores = [pltpu.make_async_copy(held[i], out[i], sems.at[1, i]) for i in range(6)]
    for i in order:
        loads[i].start()
    for i in order:
        loads[i].wait()
        stores[i].start()
    for i in order:
        stores[i].wait()


def natural_features():
    place = np.arange(ENC)
    return (160 * (place % 160 // 20) + 20 * (place // 160) + place % 20).astype(np.int32)[None]


def shards(
    frames, live_frames, enc_gain, enc_q, enc_s, text, live_text, dec_gain, val_q, val_s,
    down, up, audio_cot, text_cot,
):
    operands = (
        frames,
        live_frames.reshape(1, 1),
        enc_gain,
        enc_q,
        enc_s,
        text,
        live_text.reshape(1, 1),
        dec_gain,
        val_q,
        val_s.T,
        down,
        up.T,
        audio_cot,
        text_cot,
        jnp.asarray(natural_features()),
    )
    dma = pltpu.SemaphoreType.DMA
    vmem = pltpu.VMEM
    results = pl.pallas_call(
        kernel,
        out_shape=(
            jax.ShapeDtypeStruct((AUDIO_ROWS, VALUE), BF16),
            jax.ShapeDtypeStruct((TEXT_ROWS, VALUE), BF16),
            jax.ShapeDtypeStruct((AUDIO_ROWS, DEC), BF16),
            jax.ShapeDtypeStruct((TEXT_ROWS, DEC), BF16),
            jax.ShapeDtypeStruct((40, RANK), F32),
            jax.ShapeDtypeStruct((8, RANK), F32),
        ),
        in_specs=[pl.BlockSpec(memory_space=pltpu.HBM)] * 15,
        out_specs=[pl.BlockSpec(memory_space=vmem)] * 6,
        scratch_shapes=[
            *(vmem(a.shape, a.dtype) for a in operands),
            vmem((2, 4, Y, SLAB, 128), BF16),
            vmem((5, Z, 160, 128), BF16),
            vmem((2, Y, 32, SLAB), BF16),
            vmem((Y, 2, 3, 16, 128), BF16),
            vmem((2, 40, 128), F32),
            vmem((128, 128), F32),
            vmem((Z, 32, 128), BF16),
            vmem((2, 5, 16, 128), BF16),
            vmem((2, 3, 16, 128), BF16),
            vmem((16, ENC), F32),
            vmem((160, 128), F32),
            vmem((2, 4, 40, 128), F32),
            vmem((2, 2, 40, 128), F32),
            vmem((ROWS, VALUE), BF16),
            vmem((Y, ROWS, SLAB), F32),
            vmem((Y, ROWS, SLAB), BF16),
            vmem((Y, ROWS, SLAB), F32),
            vmem((ROWS, VALUE), F32),
            vmem((ENC // 128, 4 * AUDIO_ROWS, 128), F32),
            vmem((2, 4 * AUDIO_ROWS, ENC), BF16),
            vmem((2, 4 * AUDIO_ROWS, HALF), F32),
            vmem((2, 4 * AUDIO_ROWS, HALF), F32),
            vmem((Y, 1, SLAB), F32),
            vmem((2, Z, 16 * Y, 128), F32),
            vmem((Z, 16 * Y, 128), F32),
            vmem((Z, 16 * Y, 128), BF16),
            vmem((Z, 16 * Y, 128), BF16),
            vmem((Y, 24, 128), F32),
            vmem((Y, 24, 128), F32),
            vmem((2, Z, 8 * Y, 128), F32),
            vmem((Z, 8 * Y, 128), F32),
            vmem((Z, 8 * Y, 128), BF16),
            vmem((Z, 8 * Y, 128), BF16),
            vmem((X, 24, 128), F32),
        ]
        + [dma((15,))]
        + [
            dma(shape)
            for shape in (
                (2,), (8,), (8, 2), (8,), (2, 4, 3), (8, 2), (2,), (2, 4), (1,), (2, 4, 2), (2, 8), (8, 4),
                (2,), (8,), (8,), (8,), (4,),
            )
            for _ in range(2)
        ],
        compiler_params=pltpu.CompilerParams(
            collective_id=0, has_side_effects=True, vmem_limit_bytes=60 * 1024 * 1024
        ),
        cost_estimate=pl.CostEstimate(
            flops=2 * ROWS * (2 * DEC * VALUE + ENC * ENC), bytes_accessed=6_000_000, transcendentals=0
        ),
    )(*operands)
    return pl.pallas_call(
        hand_over,
        out_shape=tuple(jax.ShapeDtypeStruct(a.shape, a.dtype) for a in results),
        in_specs=[pl.BlockSpec(memory_space=pl.ANY)] * 6,
        out_specs=[pl.BlockSpec(memory_space=pl.ANY)] * 6,
        scratch_shapes=[*(vmem(a.shape, a.dtype) for a in results), dma((2, 6))],
        compiler_params=pltpu.CompilerParams(vmem_limit_bytes=60 * 1024 * 1024),
    )(*results)


def solution(mesh):
    both = ("dp", "fsdp")
    in_specs = (
        P(both, None), P(both), P(), P("fsdp", None), P("fsdp", None), P(both, None), P(both), P(),
        P("fsdp", None), P("fsdp", None), P("fsdp", None), P(), P(both, None), P(both, None),
    )
    out_specs = (
        P(both, None), P(both, None), P(both, None), P(both, None), P("fsdp", None), P("fsdp", None),
    )
    return jax.shard_map(shards, mesh=mesh, in_specs=in_specs, out_specs=out_specs, check_vma=False)
```

```python
import math

import jax
import jax.numpy as jnp
import numpy as np
from jax import lax
from jax.experimental import pallas as pl
from jax.experimental.pallas import tpu as pltpu
from jax.sharding import PartitionSpec as P

MESH = pl.DeviceIdType.MESH
F32 = jnp.float32
BF16 = jnp.bfloat16

EPSILON = 1e-05
ADAPTER_SCALE = 2.0
X, Y, Z = 4, 8, 8
AUDIO_ROWS, TEXT_ROWS = 32, 96
ROWS = AUDIO_ROWS + TEXT_ROWS
ENC = 1280
HALF = ENC // 2
DEC = 5120
SLAB = DEC // Y
VALUE = 1024
RANK = 64
MULTIPLIER = 1.0 / math.sqrt(X * Y * Z * 2 * ROWS)

PEERS = (1, 7, 2, 6, 3, 5, 4)


ORDER = (
    "perm", "Pe", "e00", "Pd", "Pv", "e01", "e02", "rows", "e10", "d0", "e11", "e12",
    "v00", "e20", "e21", "e22", "d1", "e30", "e31", "e32", "v01", "d2", "x00", "x01",
    "hid", "x10", "x20", "v10", "enc", "gd", "d3", "share", "v11", "za", "x11", "x21",
    "gu", "v20", "zb", "x30", "x40", "b0", "f0", "v21", "x31", "x41", "b1", "f1",
    "b2", "f2", "ya", "x50", "x60", "v30", "v31", "rx", "b3", "f3", "b4", "f4",
    "x51", "x61", "b5", "f5", "b6", "f6", "x70", "x71", "b7", "f7", "vals", "out",
    "fin",
)


def nn(a, b):
    return lax.dot_general(a, b, (((1,), (0,)), ((), ())), preferred_element_type=F32)


def nt(a, b):
    return lax.dot_general(a, b, (((1,), (1,)), ((), ())), preferred_element_type=F32)


def tn(a, b):
    return lax.dot_general(a, b, (((0,), (0,)), ((), ())), preferred_element_type=F32)


def one_hot(rows, columns, hit):
    i = lax.broadcasted_iota(jnp.int32, (rows, columns), 0)
    j = lax.broadcasted_iota(jnp.int32, (rows, columns), 1)
    return jnp.where(hit(i, j), 1.0, 0.0).astype(BF16)


def spread(blocks):
    return one_hot(blocks, blocks * 64, lambda i, j: (j >= 64 * i) & (j < 64 * i + 64))


def erf(x):
    x = jnp.clip(x, -3.832506856900711, 3.832506856900711)
    s = x * x
    p = jnp.full_like(s, 0.00022905065861350646)
    for k in (0.0034082910107109506, 0.050955695062380861, 0.18520832239976145, 1.128379143519084):
        p = p * s + k
    q = jnp.full_like(s, -1.1791602954361697e-7)
    for k in (
        0.000023547966471313185,
        0.0010179625278914885,
        0.014070470171167667,
        0.11098505178285362,
        0.49746925110067538,
        1.0,
    ):
        q = q * s + k
    return x * p / q


def kernel(
    *refs,
):
    given, refs = refs[:15], refs[15:]
    out_av, out_tv, out_ag, out_tg, out_gd, out_gu = refs[:6]
    held, refs = refs[6:21], refs[21:]
    (
        frames, live_frames, enc_gain, enc_q, enc_s, text, live_text, dec_gain, val_q, val_s,
        down, up, audio_cot, text_cot, source,
    ) = held
    (
    V, E, DT, e1, dnp, tdn, dn1, ebuf, emine, et, et2, wv, vx, cot, xs, nrm, gn, acc, enc_f, en_p,
    hall, hbuf, gain_rows,
    RA, RA2, RAs, RAr, TA, TAr, RB, RB2, RBs, RBr, FX,
    in_sem, pair_s, pair_r, p1v_s, p1v_r, p1e_s, p1e_r, p1d_s, p1d_r,
    er_s, er_r, ex_s, ex_r, hp_s, hp_r, dr_s, dr_r, dd_s, dd_r, vy_s, vy_r, vx_s, vx_r, vd_s, vd_r,
    rp_s, rp_r, za_s, za_r, zb_s, zb_r, ya_s, ya_r, rx_s, rx_r,
    ) = refs
    x = lax.axis_index("dp")
    f = lax.axis_index("fsdp")
    c = f % 2
    z = (f // 2) % Z
    y = f // (2 * Z)
    par = x % 2
    oc = 1 - c

    def dev(dx=0, dy=0, dz=0, core=None):
        return (
            (x + dx) % X if dx else x,
            (((y + dy) % Y if dy else y) * Z + ((z + dz) % Z if dz else z)) * 2
            + (c if core is None else core),
        )

    sibling = dev(core=oc)
    sent = []

    def send(src, dst, ss, rs, to):
        copy = pltpu.make_async_remote_copy(
            src_ref=src, dst_ref=dst, send_sem=ss, recv_sem=rs, device_id=to, device_id_type=MESH
        )
        copy.start()
        sent.append(copy)

    def got(dst, ss, rs):
        pltpu.make_async_remote_copy(
            src_ref=dst, dst_ref=dst, send_sem=ss, recv_sem=rs, device_id=sibling,
            device_id_type=MESH,
        ).wait_recv()

    barrier = pltpu.get_barrier_semaphore()
    peers = [sibling]
    peers += [dev(dx=k) for k in range(1, X)]
    peers += [dev(dy=k, core=core) for k in range(1, Y) for core in (c, oc)]
    peers += [dev(dz=k) for k in range(1, Z)]
    for peer in peers:
        pl.semaphore_signal(barrier, inc=1, device_id=peer, device_id_type=MESH)

    loads = [pltpu.make_async_copy(given[i], held[i], in_sem.at[i]) for i in range(15)]
    for i in (4, 3, 10, 9, 8, 0, 2, 14, 13, 12, 11, 6, 5, 7, 1):
        loads[i].start()

    def loaded(*indices):
        for i in indices:
            loads[i].wait()

    def e_index(r):
        return 2 if r == 2 else 3 * par + r

    et[...] = jnp.zeros_like(et)
    loaded(4, 3)
    et[0:10, :] = enc_q[...].astype(F32) * nn(enc_s[...], spread(ENC // 64))
    for b in range(10):
        ebuf[b // 5, b % 5] = et[:, 128 * b : 128 * b + 128].astype(BF16)
    for h in range(2):
        for r in range(3):
            emine[h, r] = ebuf[h, e_index(r)]
    e1[y, c] = emine[c]

    pl.semaphore_wait(barrier, len(peers))

    send(emine.at[oc], e1.at[y, c], p1e_s.at[0, 1], p1e_r.at[0, 1], sibling)
    for k in PEERS:
        send(emine.at[c], e1.at[y, c], p1e_s.at[k, 0], p1e_r.at[k, 0], dev(dy=k))
        send(emine.at[oc], e1.at[y, c], p1e_s.at[k, 1], p1e_r.at[k, 1], dev(dy=k, core=oc))
    loaded(10)
    dnp[c] = nn(down[...], one_hot(RANK, 128, lambda i, j: i == j))
    tdn[...] = jnp.zeros_like(tdn)
    send(dnp.at[c], dnp.at[c], pair_s.at[1], pair_r.at[1], sibling)
    loaded(9, 8)
    weight = val_q[...].astype(F32) * tn(val_s[...], spread(VALUE // 64))
    for b in range(8):
        wv[b // 4, b % 4] = weight[:, 128 * b : 128 * b + 128]
    vx[c] = wv[c, pl.ds(2 * par, 2)]
    send(wv.at[oc, pl.ds(2 * par, 2)], vx.at[c], pair_s.at[0], pair_r.at[0], sibling)

    got(dnp.at[oc], pair_s.at[1], pair_r.at[1])
    tdn[:, 0:80] = jnp.transpose(dnp[...].reshape(80, 128))
    dn1[z] = tdn[pl.ds(pl.multiple_of(32 * c, 32), 32), :].astype(BF16)
    for k in PEERS:
        send(dn1.at[z], dn1.at[z], p1d_s.at[k], p1d_r.at[k], dev(dz=k))
    got(vx.at[oc], pair_s.at[0], pair_r.at[0])
    for i in range(2):
        V[c, 2 * par + i, y, pl.ds(pl.multiple_of(80 * z, 16), 80), :] = jnp.concatenate(
            [vx[0, i], vx[1, i]], axis=0
        ).astype(BF16)

    def chip_rows(zz):
        return V.at[c, pl.ds(2 * par, 2), y, pl.ds(pl.multiple_of(80 * zz, 16), 80)]

    for k in PEERS:
        send(chip_rows(z), chip_rows(z), p1v_s.at[k], p1v_r.at[k], dev(dz=k))

    def e_part(s, d, way, r):
        return E.at[e_index(r), s] if d < 3 else E.at[e_index(r), s, pl.ds(80 * way, 80)]

    def e_send(way, d, r):
        s = (z + 8 - d) % Z if way == 0 else (z + d) % Z
        part = e_part(s, d, way, r)
        send(part, part, er_s.at[way, d, r], er_r.at[way, d, r], dev(dz=1 if way == 0 else 7))

    def e_across(s, n, r):
        if r < 2:
            send(E.at[e_index(r), s], E.at[e_index(r), s], ex_s.at[n, r], ex_r.at[n, r], dev(dx=1 if r == 0 else 3))

    def e_step(d, r):
        for way in range(2):
            s = (z + 7 - d) % Z if way == 0 else (z + 1 + d) % Z
            got(e_part(s, d, way, r), er_s.at[way, d, r], er_r.at[way, d, r])
            if d < 3:
                e_send(way, d + 1, r)
                e_across(s, 1 + 2 * d + way, r)
        if d == 3:
            e_across((z + 4) % Z, 7, r)

    def v_blk(s, i):
        return V.at[c, 2 * par + i, s]

    def x_blk(s, i):
        return V.at[c, 2 * (1 - par) + i, s]

    def v_half(q, s, j):
        return V.at[c, q, s, pl.ds(320 * j, 320)]

    def v_send(way, d, i):
        s = (y + 8 - d) % Y if way == 0 else (y + d) % Y
        to = dev(dy=1 if way == 0 else 7)
        if d < 3:
            send(v_blk(s, i), v_blk(s, i), vy_s.at[way, d, i], vy_r.at[way, d, i], to)
        else:
            for j in range(2):
                part = v_half(2 * par + i, s, j)
                send(part, part, vy_s.at[way, d, j], vy_r.at[way, d, j], to)

    def v_spread(part, n, i):
        right = i == 0 if n in (0, 7, 8) else i == (n + 1) % 2
        send(part, part, vx_s.at[i, n], vx_r.at[i, n], dev(dx=1 if right else 3))
        send(part, part, vd_s.at[n, i], vd_r.at[n, i], sibling)

    def v_step(d, i):
        for way in range(2):
            s = (y + 7 - d) % Y if way == 0 else (y + 1 + d) % Y
            if d < 3:
                got(v_blk(s, i), vy_s.at[way, d, i], vy_r.at[way, d, i])
                if d < 2 or way == i:
                    v_send(way, d + 1, i)
                v_spread(v_blk(s, i), 1 + 2 * d + way, i)
            else:
                part = v_half(2 * par + way, s, i)
                got(part, vy_s.at[way, d, i], vy_r.at[way, d, i])
                v_spread(part, 7 + i, way)

    def slab_of(n):
        d = (n + 1) // 2
        return (y + 8 - d) % Y if n % 2 == 1 else (y + d) % Y

    def x_step(n, i):
        if n < 7:
            takes = ((x_blk(slab_of(n), i), n, i),)
        else:
            takes = tuple((v_half(2 * (1 - par) + b, slab_of(7), i), 7 + i, b) for b in range(2))
        for part, at, b in takes:
            got(part, vx_s.at[b, at], vx_r.at[b, at])
            send(part, part, vd_s.at[at, 2 + b], vd_r.at[at, 2 + b], sibling)

    def ready(n):
        s = slab_of(n)
        for i in range(2):
            for q, b in ((2 * par + i, i), (2 * (1 - par) + i, 2 + i)):
                if n < 7:
                    got(V.at[oc, q, s], vd_s.at[n, b], vd_r.at[n, b])
                else:
                    for j in range(2):
                        got(V.at[oc, q, s, pl.ds(320 * j, 320)], vd_s.at[7 + j, b], vd_r.at[7 + j, b])

    def d_slab(s, d, way):
        return DT.at[c, s] if d < 3 else DT.at[c, s, pl.ds(16 * way, 16)]

    def d_send(d):
        send(d_slab((y + 8 - d) % Y, d, 0), d_slab((y + 8 - d) % Y, d, 0), dr_s.at[0, d], dr_r.at[0, d], dev(dy=1))
        send(d_slab((y + d) % Y, d, 1), d_slab((y + d) % Y, d, 1), dr_s.at[1, d], dr_r.at[1, d], dev(dy=7))

    def d_step(d):
        got(d_slab((y + 7 - d) % Y, d, 0), dr_s.at[0, d], dr_r.at[0, d])
        got(d_slab((y + 1 + d) % Y, d, 1), dr_s.at[1, d], dr_r.at[1, d])
        if d < 3:
            d_send(d + 1)

    state = {}

    def whole(s):
        return jnp.concatenate([V[b // 4, b % 4, s] for b in range(8)], axis=1)

    def backward(n):
        s = slab_of(n)
        gn[s] = nt(cot[...], whole(s))

    def forward(n):
        s = slab_of(n)
        product = nn(nrm[s], whole(s))
        acc[...] = product if n == 0 else acc[...] + product
        adapter = nn(state["bl"], jnp.concatenate([DT[0, s], DT[1, s]], axis=0))
        u = (gn[s] + adapter) * gain_rows[s]
        gn[s] = u
        part = jnp.sum(u * xs[s], axis=1, keepdims=True)
        state["mean"] = part if n == 0 else state["mean"] + part


    def twice():
        return one_hot(RANK, 128, lambda i, j: (j == i) | (j == i + RANK))

    def first(height):
        return lax.broadcasted_iota(jnp.int32, (height, 128), 1) < RANK

    def share_d():
        send(DT.at[c], DT.at[c], dd_s.at[0], dd_r.at[0], sibling)

    def do_start_e():
        got(e1.at[y, oc], p1e_s.at[0, 1], p1e_r.at[0, 1])
        for k in PEERS:
            got(e1.at[(y + 8 - k) % Y, c], p1e_s.at[k, 0], p1e_r.at[k, 0])
            got(e1.at[(y + 8 - k) % Y, oc], p1e_s.at[k, 1], p1e_r.at[k, 1])
        for r in range(3):
            for yy in range(Y):
                for cc in range(2):
                    et2[20 * yy + 10 * cc : 20 * yy + 10 * cc + 10, :] = e1[yy, cc, r].astype(F32)[0:10]
            E[e_index(r), z] = et2[...].astype(BF16)

        for r in range(3):
            e_send(0, 0, r)
            e_send(1, 0, r)
            e_across(z, 0, r)

    def do_start_v():
        for k in PEERS:
            got(chip_rows((z + 8 - k) % Z), p1v_s.at[k], p1v_r.at[k])

        for i in range(2):
            v_send(0, 0, i)
            v_send(1, 0, i)
            v_spread(v_blk(y, i), 0, i)

    def do_start_d():
        for k in PEERS:
            got(dn1.at[(z + 8 - k) % Z], p1d_s.at[k], p1d_r.at[k])
        DT[c, y] = jnp.concatenate([dn1[k].astype(F32)[:, 0:80] for k in range(Z)], axis=1).astype(BF16)

        d_send(0)

    def do_perm():
        loaded(0, 2, 14)
        signal = frames[...].astype(F32)
        center = signal - jnp.mean(signal, axis=1, keepdims=True)
        variance = jnp.mean(center * center, axis=1, keepdims=True)
        en = (center * lax.rsqrt(variance + EPSILON) * enc_gain[...].astype(F32).reshape(1, ENC)).astype(BF16)
        feature = lax.broadcasted_iota(jnp.int32, (ENC, 128), 0)
        for b in range(ENC // 128):
            cols = slice(128 * b, 128 * b + 128)
            pick = jnp.where(feature == source[:, cols], 1.0, 0.0).astype(BF16)
            en_p[c, :, cols] = nn(en, pick).astype(BF16)
        send(en_p.at[c], en_p.at[c], hp_s.at[0], hp_r.at[0], sibling)

    def do_rows():
        loaded(13, 12, 11, 6, 5, 7, 1)
        cot[0:AUDIO_ROWS, :] = audio_cot[...]
        row = lax.broadcasted_iota(jnp.int32, (TEXT_ROWS, 1), 0)
        mask = jnp.where(row < live_text[...], 1.0, 0.0)
        cot[AUDIO_ROWS:ROWS, :] = (text_cot[...].astype(F32) * mask).astype(BF16)
        state["bl"] = (ADAPTER_SCALE * nt(cot[...], up[...])).astype(BF16)
        gains = [dec_gain[SLAB * k : SLAB * (k + 1)].astype(F32).reshape(1, SLAB) for k in range(Y)]
        for k in range(Y):
            gain_rows[k] = gains[k]
        square = jnp.zeros((TEXT_ROWS, 1), F32)
        for k in range(Y):
            part = text[:, SLAB * k : SLAB * (k + 1)].astype(F32)
            square += jnp.sum(part * part, axis=1, keepdims=True)
        state["inv_text"] = inv_text = lax.rsqrt(square * (1.0 / DEC) + EPSILON)
        for k in range(Y):
            part = text[:, SLAB * k : SLAB * (k + 1)].astype(F32)
            xs[k, AUDIO_ROWS:ROWS, :] = part
            nrm[k, AUDIO_ROWS:ROWS, :] = (part * inv_text * gains[k]).astype(BF16)

    def do_hid():
        for n in range(8):
            d = (n + 1) // 2
            s = (z + 8 - d) % Z if n % 2 == 1 else (z + d) % Z
            for r in range(2):
                got(E.at[3 * (1 - par) + r, s], ex_s.at[n, r], ex_r.at[n, r])
        got(en_p.at[oc], hp_s.at[0], hp_r.at[0])
        mine = jnp.concatenate([E[b].reshape(ENC, 128) for b in range(5)], axis=1)
        hbuf[...] = nn(en_p[...].reshape(8 * AUDIO_ROWS, ENC), mine).reshape(2, 4 * AUDIO_ROWS, HALF)
        send(hbuf.at[oc], hall.at[c], hp_s.at[1], hp_r.at[1], sibling)
        hall[c] = hbuf[c]

    def do_enc():
        got(hall.at[oc], hp_s.at[1], hp_r.at[1])
        frame = lax.broadcasted_iota(jnp.int32, (4 * AUDIO_ROWS, 1), 0)
        live = jnp.where(frame < live_frames[...], 1.0, 0.0)
        for h in range(2):
            cols = slice(HALF * h, HALF * (h + 1))
            hidden = hall[h]
            gelu = 0.5 * hidden * (1.0 + erf(hidden * (1.0 / math.sqrt(2.0))))
            encoded = ((frames[:, cols].astype(F32) + gelu) * live).astype(BF16)
            for b in range(5):
                enc_f[5 * h + b] = encoded[:, 128 * b : 128 * b + 128].astype(F32)
        square = jnp.zeros((AUDIO_ROWS, 1), F32)
        for k in range(4):
            for b in range(10):
                part = enc_f[b, pl.ds(k, AUDIO_ROWS, stride=4), :]
                square += jnp.sum(part * part, axis=1, keepdims=True)
                xs[2 * k + b // 5, 0:AUDIO_ROWS, 128 * (b % 5) : 128 * (b % 5) + 128] = part
        state["inv_audio"] = inv_audio = lax.rsqrt(square * (1.0 / DEC) + EPSILON)
        for k in range(Y):
            nrm[k, 0:AUDIO_ROWS, :] = (xs[k, 0:AUDIO_ROWS, :] * inv_audio * gain_rows[k]).astype(BF16)

    def do_gd():
        bl2 = nn(state["bl"], twice()).astype(BF16)
        for k in range(Y):
            g_down = tn(nrm[k], bl2) * MULTIPLIER
            for zz in range(Z):
                for cc in range(2):
                    at = 80 * zz + 40 * cc
                    RA[cc, zz, 16 * k : 16 * k + 16, :] = jnp.where(
                        first(16), g_down[at : at + 16], g_down[at + 24 : at + 40]
                    )
                    RB[cc, zz, 8 * k : 8 * k + 8, :] = g_down[at + 16 : at + 24]
        send(RA.at[oc], RA2, rp_s.at[0], rp_r.at[0], sibling)

    def do_gu():
        got(DT.at[oc], dd_s.at[0], dd_r.at[0])
        low = jnp.zeros((ROWS, RANK), F32)
        for k in range(Y):
            low += nt(nrm[k], jnp.concatenate([DT[0, k], DT[1, k]], axis=0))
        state["lr"] = lr = low.astype(BF16)
        lr2 = nn(lr, twice()).astype(BF16)
        g_up = tn(cot[...], lr2) * (ADAPTER_SCALE * MULTIPLIER)
        for k in range(Y):
            for zz in range(Z):
                for cc in range(2):
                    u = 16 * (Z * k + zz) + 8 * cc
                    part = RB[cc, zz, 8 * k : 8 * k + 8, :]
                    RB[cc, zz, 8 * k : 8 * k + 8, :] = jnp.where(first(8), part, g_up[u : u + 8])
        send(RB.at[oc], RB2, rp_s.at[1], rp_r.at[1], sibling)

    def do_za():
        got(RA2, rp_s.at[0], rp_r.at[0])
        for k in PEERS:
            at = (z + k) % Z
            RAs[at] = (RA[c, at] + RA2[at]).astype(BF16)
            send(RAs.at[at], RAr.at[k], za_s.at[k], za_r.at[k], dev(dz=k))

    def do_zb():
        got(RB2, rp_s.at[1], rp_r.at[1])
        for k in PEERS:
            at = (z + k) % Z
            RBs[at] = (RB[c, at] + RB2[at]).astype(BF16)
            send(RBs.at[at], RBr.at[k], zb_s.at[k], zb_r.at[k], dev(dz=k))

    def do_ya():
        part_a, part_b = RA[c, z] + RA2[z], RB[c, z] + RB2[z]
        for k in PEERS:
            got(RAr.at[k], za_s.at[k], za_r.at[k])
            part_a += RAr[k].astype(F32)
        for k in PEERS:
            got(RBr.at[k], zb_s.at[k], zb_r.at[k])
            part_b += RBr[k].astype(F32)
        for yy in range(Y):
            TA[yy, 0:16, :] = part_a[16 * yy : 16 * yy + 16]
            TA[yy, 16:24, :] = part_b[8 * yy : 8 * yy + 8]
        for k in PEERS:
            send(TA.at[(y + k) % Y], TAr.at[k], ya_s.at[k], ya_r.at[k], dev(dy=k))

    def do_rx():
        total = TA[y]
        for k in PEERS:
            got(TAr.at[k], ya_s.at[k], ya_r.at[k])
            total += TAr[k]
        FX[x] = total
        for k in range(1, X):
            send(FX.at[x], FX.at[x], rx_s.at[k], rx_r.at[k], dev(dx=k))

    def do_vals():
        values = (acc[...] + ADAPTER_SCALE * nn(state["lr"], up[...])).astype(BF16)
        out_av[...] = values[0:AUDIO_ROWS]
        out_tv[...] = values[AUDIO_ROWS:ROWS]
        inverse = jnp.concatenate([state["inv_audio"], state["inv_text"]], axis=0)
        state["inverse"] = inverse

    def do_out():
        inverse, mean = state["inverse"], state["mean"]
        scale = inverse * inverse * inverse * (mean * (1.0 / DEC))
        for k in range(Y):
            cols = slice(SLAB * k, SLAB * (k + 1))
            grad = (inverse * gn[k] - xs[k] * scale).astype(BF16)
            out_ag[:, cols] = grad[0:AUDIO_ROWS]
            out_tg[:, cols] = grad[AUDIO_ROWS:ROWS]

    def do_fin():
        for k in range(1, X):
            got(FX.at[(x + 4 - k) % X], rx_s.at[k], rx_r.at[k])
        total = FX[0] + FX[1] + FX[2] + FX[3]
        right = pltpu.roll(total, RANK, axis=1)
        out_gd[0:24, :] = total[:, :RANK]
        out_gd[24:40, :] = right[0:16, :RANK]
        out_gu[...] = right[16:24, :RANK]

    def slab(n):
        ready(n)
        backward(n)

    named = {
        "Pe": do_start_e, "Pv": do_start_v, "Pd": do_start_d, "perm": do_perm, "rows": do_rows, "hid": do_hid,
        "enc": do_enc, "gd": do_gd, "gu": do_gu, "za": do_za, "zb": do_zb, "ya": do_ya, "rx": do_rx, "vals": do_vals, "out": do_out,
        "fin": do_fin, "share": share_d,
    }
    steps = {"e": e_step, "d": d_step, "v": v_step, "x": x_step, "b": slab, "f": forward}
    for step in ORDER:
        if step in named:
            named[step]()
        else:
            steps[step[0]](*(int(digit) for digit in step[1:]))

    for copy in sent:
        copy.wait_send()


def hand_over(*refs):
    given, out, held, sems = refs[:6], refs[6:12], refs[12:18], refs[18]
    order = (3, 2, 1, 0, 4, 5)
    loads = [pltpu.make_async_copy(given[i], held[i], sems.at[0, i]) for i in range(6)]
    stores = [pltpu.make_async_copy(held[i], out[i], sems.at[1, i]) for i in range(6)]
    for i in order:
        loads[i].start()
    for i in order:
        loads[i].wait()
        stores[i].start()
    for i in order:
        stores[i].wait()


def natural_features():
    place = np.arange(ENC)
    return (160 * (place % 160 // 20) + 20 * (place // 160) + place % 20).astype(np.int32)[None]


def shards(
    frames, live_frames, enc_gain, enc_q, enc_s, text, live_text, dec_gain, val_q, val_s,
    down, up, audio_cot, text_cot,
):
    operands = (
        frames,
        live_frames.reshape(1, 1),
        enc_gain,
        enc_q,
        enc_s,
        text,
        live_text.reshape(1, 1),
        dec_gain,
        val_q,
        val_s.T,
        down,
        up.T,
        audio_cot,
        text_cot,
        jnp.asarray(natural_features()),
    )
    dma = pltpu.SemaphoreType.DMA
    vmem = pltpu.VMEM
    results = pl.pallas_call(
        kernel,
        out_shape=(
            jax.ShapeDtypeStruct((AUDIO_ROWS, VALUE), BF16),
            jax.ShapeDtypeStruct((TEXT_ROWS, VALUE), BF16),
            jax.ShapeDtypeStruct((AUDIO_ROWS, DEC), BF16),
            jax.ShapeDtypeStruct((TEXT_ROWS, DEC), BF16),
            jax.ShapeDtypeStruct((40, RANK), F32),
            jax.ShapeDtypeStruct((8, RANK), F32),
        ),
        in_specs=[pl.BlockSpec(memory_space=pltpu.HBM)] * 15,
        out_specs=[pl.BlockSpec(memory_space=vmem)] * 6,
        scratch_shapes=[
            *(vmem(a.shape, a.dtype) for a in operands),
            vmem((2, 4, Y, SLAB, 128), BF16),
            vmem((5, Z, 160, 128), BF16),
            vmem((2, Y, 32, SLAB), BF16),
            vmem((Y, 2, 3, 16, 128), BF16),
            vmem((2, 40, 128), F32),
            vmem((128, 128), F32),
            vmem((Z, 32, 128), BF16),
            vmem((2, 5, 16, 128), BF16),
            vmem((2, 3, 16, 128), BF16),
            vmem((16, ENC), F32),
            vmem((160, 128), F32),
            vmem((2, 4, 40, 128), F32),
            vmem((2, 2, 40, 128), F32),
            vmem((ROWS, VALUE), BF16),
            vmem((Y, ROWS, SLAB), F32),
            vmem((Y, ROWS, SLAB), BF16),
            vmem((Y, ROWS, SLAB), F32),
            vmem((ROWS, VALUE), F32),
            vmem((ENC // 128, 4 * AUDIO_ROWS, 128), F32),
            vmem((2, 4 * AUDIO_ROWS, ENC), BF16),
            vmem((2, 4 * AUDIO_ROWS, HALF), F32),
            vmem((2, 4 * AUDIO_ROWS, HALF), F32),
            vmem((Y, 1, SLAB), F32),
            vmem((2, Z, 16 * Y, 128), F32),
            vmem((Z, 16 * Y, 128), F32),
            vmem((Z, 16 * Y, 128), BF16),
            vmem((Z, 16 * Y, 128), BF16),
            vmem((Y, 24, 128), F32),
            vmem((Y, 24, 128), F32),
            vmem((2, Z, 8 * Y, 128), F32),
            vmem((Z, 8 * Y, 128), F32),
            vmem((Z, 8 * Y, 128), BF16),
            vmem((Z, 8 * Y, 128), BF16),
            vmem((X, 24, 128), F32),
        ]
        + [dma((15,))]
        + [
            dma(shape)
            for shape in (
                (2,), (8,), (8, 2), (8,), (2, 4, 3), (8, 2), (2,), (2, 4), (1,), (2, 4, 2), (2, 9), (9, 4),
                (2,), (8,), (8,), (8,), (4,),
            )
            for _ in range(2)
        ],
        compiler_params=pltpu.CompilerParams(
            collective_id=0, has_side_effects=True, vmem_limit_bytes=60 * 1024 * 1024
        ),
        cost_estimate=pl.CostEstimate(
            flops=2 * ROWS * (2 * DEC * VALUE + ENC * ENC), bytes_accessed=6_000_000, transcendentals=0
        ),
    )(*operands)
    return pl.pallas_call(
        hand_over,
        out_shape=tuple(jax.ShapeDtypeStruct(a.shape, a.dtype) for a in results),
        in_specs=[pl.BlockSpec(memory_space=pl.ANY)] * 6,
        out_specs=[pl.BlockSpec(memory_space=pl.ANY)] * 6,
        scratch_shapes=[*(vmem(a.shape, a.dtype) for a in results), dma((2, 6))],
        compiler_params=pltpu.CompilerParams(vmem_limit_bytes=60 * 1024 * 1024),
    )(*results)


def solution(mesh):
    both = ("dp", "fsdp")
    in_specs = (
        P(both, None), P(both), P(), P("fsdp", None), P("fsdp", None), P(both, None), P(both), P(),
        P("fsdp", None), P("fsdp", None), P("fsdp", None), P(), P(both, None), P(both, None),
    )
    out_specs = (
        P(both, None), P(both, None), P(both, None), P(both, None), P("fsdp", None), P("fsdp", None),
    )
    return jax.shard_map(shards, mesh=mesh, in_specs=in_specs, out_specs=out_specs, check_vma=False)
```
